512 devices in a mesh: patch: 64 (over y, x, core), band: 8 (over z).
Axes of the slice: x: 4, y: 8, z: 8, core: 2. Of those that a mesh axis runs over, the one named last changes fastest.
Arguments:
- nodes: bfloat16 [65536, 512], P(('patch', 'band')), may hold values from -6 to 6
- edges: bfloat16 [393216, 512], P(('patch', 'band')), may hold values from -6 to 6
- d_new_edges: bfloat16 [393216, 512], P(('patch', 'band')), may hold values from -6 to 6
- d_aggregate: bfloat16 [65536, 512], P(('patch', 'band')), may hold values from -6 to 6
- edge_w1: bfloat16 [1536, 512], replicated, may hold values from -0.15625 to 0.15625
- edge_w2: bfloat16 [512, 512], replicated, may hold values from -0.25 to 0.25
- senders: int32 [393216], P(('patch', 'band')), may hold values from 0 to 65535, as said below
- receivers: int32 [393216], P(('patch', 'band')), may hold values from 0 to 127
- edge_count: int32 [512], P(('patch', 'band')), may hold values from 307 to 768, as said below
Outputs:
- d_nodes: bfloat16 [65536, 512], P(('patch', 'band'))
- d_edges: bfloat16 [393216, 512], P(('patch', 'band'))
- d_edge_w1: float32 [1536, 512], P('patch')
The draws below stay inside these ranges and needn't reach their ends.
Inputs may be any that keep to these rules, and one draw needn't show every extreme that they name: `senders`: each sender has the band of its edge slot's device and lies in that slot's device, among the last 32 nodes of the device one patch lower, or among the first 32 nodes of the device one patch higher (patches taken cyclically). `edge_count`: some device has all 768 slots live.
All inputs are finite; a program needn't handle non-finite values.
Results may differ from the reference program's by a relative error of at most 0.017.
Values may be sent and summed in bfloat16 or wider, within the bound.
No kernel may reach another device: no remote copies, remote signals or barrier semaphores. Data moves between devices by JAX's collectives and lax.ppermute only.
A program may use at most 64 MiB of HBM per device.

```python
import jax
import jax.numpy as jnp
from jax import lax

D = 512
M_DEV = 128
E_DEV = 768
HALO = 32
NODES = 65536
EDGES = 393216
N_PATCH = 64
N_BAND = 8


def draw_senders(key, part):
    key = jax.random.fold_in(key, 11)
    first, second, third = jax.random.split(key, 3)
    index = jnp.arange(EDGES, dtype=jnp.int32)
    owner = index // E_DEV
    patch = owner // N_BAND
    band = owner % N_BAND
    kind = jax.random.randint(first, (EDGES,), 0, 4)
    near = jax.random.randint(second, (EDGES,), 0, HALO)
    anywhere = jax.random.randint(third, (EDGES,), 0, M_DEV)
    lower = (patch - 1) % N_PATCH
    upper = (patch + 1) % N_PATCH
    source = jnp.where(kind == 0, lower, jnp.where(kind == 1, upper, patch))
    offset = jnp.where(kind == 0, M_DEV - HALO + near, jnp.where(kind == 1, near, anywhere))
    return ((source * N_BAND + band) * M_DEV + offset).astype(jnp.int32)


def draw_edge_count(key, part):
    key = jax.random.fold_in(key, 12)
    first, second = jax.random.split(key, 2)
    total = N_PATCH * N_BAND
    counts = jax.random.randint(first, (total,), 2 * E_DEV // 5, E_DEV + 1)
    chosen = jax.random.randint(second, (), 0, total)
    return jnp.where(jnp.arange(total) == chosen, E_DEV, counts).astype(jnp.int32)


def plant(values, rng, least, top_value):
    longest = values.shape.index(max(values.shape))
    spots = []
    for shift in (0, 1):
        where = [jax.random.randint(jax.random.fold_in(rng, axis), (), 0, length) for axis, length in enumerate(values.shape)]
        where[longest] = (where[longest] + shift) % values.shape[longest]
        spots.append(tuple(where))
    return values.at[spots[0]].set(least).at[spots[1]].set(top_value)


def block_scale(key, extent, pieces, smallest, top_value):
    factor_of = 1.0
    for position, blocks in pieces:
        draws = jax.random.uniform(jax.random.fold_in(jax.random.fold_in(key, 6), position), (blocks,), jnp.float32, smallest / len(pieces), top_value / len(pieces))
        factor_of = factor_of * jnp.repeat(jnp.exp(draws), extent[position] // blocks).reshape((-1,) + (1,) * (len(extent) - 1 - position))
    return factor_of


def centred(stream_key, dims, spread, limit, cuts=(), held_as=jnp.bfloat16):
    loudness = block_scale(stream_key, dims, cuts, -0.22, 0.18) if cuts else 1.0
    values = jax.random.normal(stream_key, dims, jnp.float32) * spread * loudness
    return jnp.minimum(jnp.maximum(values, -limit), limit).astype(held_as)


def setup_inputs(seed: int = 0) -> dict:
    streams_of = jax.random.split(jax.random.key(seed), 10)
    return {
        "nodes": centred(streams_of[0], (NODES, D), 1.0, 6.0, ((0, 512),)),
        "edges": centred(streams_of[1], (EDGES, D), 1.0, 6.0, ((0, 512),)),
        "d_new_edges": centred(streams_of[2], (EDGES, D), 1.0, 6.0, ((0, 512),)),
        "d_aggregate": centred(streams_of[3], (NODES, D), 1.0, 6.0, ((0, 512),)),
        "edge_w1": centred(streams_of[4], (3 * D, D), (3 * D) ** -0.5, 0.15625),
        "edge_w2": centred(streams_of[5], (D, D), D ** -0.5, 0.25),
        "senders": draw_senders(jax.random.fold_in(streams_of[9], 71), 0),
        "receivers": plant(jax.random.randint(streams_of[7], (EDGES,), 0, M_DEV), jax.random.fold_in(streams_of[7], 1), 0, M_DEV - 1).astype(jnp.int32),
        "edge_count": draw_edge_count(jax.random.fold_in(streams_of[9], 71), 0),
    }


def edge_grads(stacked, grad_new, edge_w1, edge_w2):
    pre = jnp.dot(stacked, edge_w1, preferred_element_type=jnp.float32)
    hidden = jax.nn.silu(pre).astype(jnp.bfloat16)
    out = jnp.dot(hidden, edge_w2, preferred_element_type=jnp.float32)
    center = out - lax.optimization_barrier(jnp.mean(out, axis=-1, keepdims=True))
    rstd = lax.rsqrt(lax.optimization_barrier(jnp.mean(center * center, axis=-1, keepdims=True)) + 1e-05)
    normed = center * rstd
    g_out = (grad_new - lax.optimization_barrier(jnp.mean(grad_new, axis=-1, keepdims=True)) - normed * lax.optimization_barrier(jnp.mean(grad_new * normed, axis=-1, keepdims=True))) * rstd
    g_out = g_out.astype(jnp.bfloat16)
    g_hidden = lax.dot_general(g_out, edge_w2, (((1,), (1,)), ((), ())), preferred_element_type=jnp.float32)
    sigma = jax.nn.sigmoid(pre)
    dz = (g_hidden * sigma * (1.0 + pre * (1.0 - sigma))).astype(jnp.bfloat16)
    grad_in = lax.dot_general(dz, edge_w1, (((1,), (1,)), ((), ())), preferred_element_type=jnp.float32)
    return (dz, grad_in)

def reference(nodes, edges, d_new_edges, d_aggregate, edge_w1, edge_w2, senders, receivers, edge_count):
    blocks = N_PATCH * N_BAND
    edge_blocks = edges.reshape(blocks, E_DEV, D)
    grad_blocks = d_new_edges.reshape(blocks, E_DEV, D)
    send_blocks = senders.reshape(blocks, E_DEV)
    recv_blocks = receivers.reshape(blocks, E_DEV)
    block_ids = jnp.arange(blocks, dtype=jnp.int32)

    def step(carry, item):
        node_grad, weight_grad = carry
        block, edge_rows, grad_rows, send_rows, recv_rows, count = item
        recv_global = (block * M_DEV + recv_rows).astype(jnp.int32)
        stacked = jnp.concatenate([edge_rows, nodes[send_rows], nodes[recv_global]], axis=1)
        live = (jnp.arange(E_DEV, dtype=jnp.int32) < count).astype(jnp.float32)[:, None]
        grad_new = live * (grad_rows.astype(jnp.float32) + d_aggregate[recv_global].astype(jnp.float32))
        dz, grad_in = edge_grads(stacked, grad_new, edge_w1, edge_w2)
        node_grad = node_grad.at[send_rows].add(grad_in[:, D:2 * D])
        node_grad = node_grad.at[recv_global].add(grad_in[:, 2 * D:])
        weight_grad = weight_grad + lax.dot_general(stacked, dz, (((0,), (0,)), ((), ())), preferred_element_type=jnp.float32)
        return ((node_grad, weight_grad), (grad_new + grad_in[:, :D]).astype(jnp.bfloat16))
    start = (jnp.zeros((NODES, D), jnp.float32), jnp.zeros((3 * D, D), jnp.float32))
    (node_grad, weight_grad), edge_grad = lax.scan(step, start, (block_ids, edge_blocks, grad_blocks, send_blocks, recv_blocks, edge_count))
    return (node_grad.astype(jnp.bfloat16), edge_grad.reshape(EDGES, D), weight_grad)
```

```python
import itertools

import jax
import jax.numpy as jnp
from jax import lax
from jax.experimental import pallas as pl
from jax.experimental.pallas import tpu as pltpu
from jax.sharding import PartitionSpec as P

HALO = 32
ROWS = 128
SLOTS = 768
WIDTH = 512
BLOCK = 256
AXES = ("patch", "band")
BF16 = jnp.bfloat16
F32 = jnp.float32


def device_groups(y_parts, x_parts, z_parts):
    groups = []
    for ys, xs, zs, core in itertools.product(y_parts, x_parts, z_parts, range(2)):
        groups.append(
            [((y * 4 + x) * 2 + core) * 8 + z for x, y, z in itertools.product(xs, ys, zs)]
        )
    return groups


SINGLE_X, SINGLE_Y, SINGLE_Z = ([[i] for i in range(n)] for n in (4, 8, 8))
X_AND_Y_PAIR = device_groups([[2 * i, 2 * i + 1] for i in range(4)], [list(range(4))], SINGLE_Z)
Y_QUADS = device_groups([[0, 2, 4, 6], [1, 3, 5, 7]], SINGLE_X, SINGLE_Z)
Z_ALL = device_groups(SINGLE_Y, SINGLE_X, [list(range(8))])
PAIR = [(i, i ^ 1) for i in range(64)]
CROSS = [(i, (i - 1) % 64 if i % 2 == 0 else (i + 1) % 64) for i in range(64)]


def dot(a, b, dims):
    return lax.dot_general(a, b, (dims, ((), ())), preferred_element_type=F32)


NN = ((1,), (0,))
NT = ((1,), (1,))
TN = ((0,), (0,))


def kernel(
    scalars,
    senders,
    receivers,
    nodes,
    pair,
    cross,
    edges,
    d_new,
    d_agg,
    w1,
    w2,
    mine,
    theirs,
    d_edges,
    node_grad,
    ret_pair,
    ret_cross,
    dz_all,
    scatter,
    table,
    weight,
):
    here, odd, count = scalars[0], scalars[1], scalars[2]
    table[:ROWS] = nodes[...]
    table[ROWS : ROWS + HALO] = pair[...]
    table[ROWS + HALO :] = cross[...]
    owner = senders[...] // (ROWS * 8)
    offset = senders[...] % ROWS
    lower = jnp.where(here == 0, 63, here - 1)
    lower_base = jnp.where(odd == 1, ROWS, ROWS + HALO) - (ROWS - HALO)
    upper_base = jnp.where(odd == 1, ROWS + HALO, ROWS)
    position = jnp.where(
        owner == here, offset, jnp.where(owner == lower, lower_base + offset, upper_base + offset)
    )
    receive = receivers[...]

    def columns(index, part):
        row = jnp.broadcast_to(index[part : part + 1, :], (128, 128))
        return row.T

    def hot(mask):
        return jnp.where(mask, 1.0, 0.0).astype(BF16)

    lane = lax.broadcasted_iota(jnp.int32, (128, 128), 1)
    wide = lax.broadcasted_iota(jnp.int32, (128, 64), 1)
    for start in range(0, SLOTS, BLOCK):
        send_hot, recv_hot = [], []
        for part in range(start // 128, (start + BLOCK) // 128):
            place = columns(position, part)
            send_hot.append(
                jnp.concatenate([hot(place == lane), hot(place[:, :64] == wide + 128)], axis=1)
            )
            recv_hot.append(hot(columns(receive, part) == lane))
            row = pl.ds(part * 128, 128)
            scatter[: ROWS + 2 * HALO, row] = hot(
                lax.broadcasted_iota(jnp.int32, (192, 128), 0) == position[part : part + 1, :]
            )
            scatter[ROWS + 2 * HALO :, row] = hot(
                lax.broadcasted_iota(jnp.int32, (128, 128), 0) == receive[part : part + 1, :]
            )
        send_hot = jnp.concatenate(send_hot, axis=0)
        recv_hot = jnp.concatenate(recv_hot, axis=0)
        rows = pl.ds(start, BLOCK)
        sent = dot(send_hot, table[...], NN).astype(BF16)
        got = dot(recv_hot, nodes[...], NN).astype(BF16)
        pre = (
            dot(edges[rows, :], w1[:WIDTH], NN)
            + dot(sent, w1[WIDTH : 2 * WIDTH], NN)
            + dot(got, w1[2 * WIDTH :], NN)
        )
        sigma = 0.5 * jnp.tanh(0.5 * pre) + 0.5
        hidden = (pre * sigma).astype(BF16)
        out = dot(hidden, w2[...], NN)
        center = out - jnp.mean(out, axis=-1, keepdims=True)
        rstd = lax.rsqrt(jnp.mean(center * center, axis=-1, keepdims=True) + 1e-05)
        normed = center * rstd
        slot = start + lax.broadcasted_iota(jnp.int32, (BLOCK, 1), 0)
        live = jnp.where(slot < count, 1.0, 0.0)
        grad_new = live * (d_new[rows, :].astype(F32) + dot(recv_hot, d_agg[...], NN))
        g_out = (
            grad_new
            - jnp.mean(grad_new, axis=-1, keepdims=True)
            - normed * jnp.mean(grad_new * normed, axis=-1, keepdims=True)
        ) * rstd
        g_hidden = dot(g_out.astype(BF16), w2[...], NT)
        dz = (g_hidden * (sigma * (1.0 + pre * (1.0 - sigma)))).astype(BF16)
        dz_all[rows, :] = dz
        d_edges[rows, :] = (grad_new + dot(dz, w1[:WIDTH], NT)).astype(BF16)

    dz = dz_all[...]
    summed = dot(scatter[...], dz, NN).astype(BF16)
    by_sender, by_receiver = summed[: ROWS + 2 * HALO], summed[ROWS + 2 * HALO :]
    weight[:WIDTH] = dot(edges[...], dz, TN)
    weight[WIDTH : 2 * WIDTH] = dot(table[...], by_sender, TN)
    weight[2 * WIDTH :] = dot(nodes[...], by_receiver, TN)

    def arrange(core, target):
        for x, y in itertools.product(range(4), range(2)):
            pieces = []
            for quad in range(4):
                first = ((quad * 2 + y) * 4 + x) * 48 + core * 24
                pieces.append(weight[first : first + 24, :])
            place = (x * 2 + y) * 96
            target[place : place + 96, :] = jnp.concatenate(pieces, axis=0).astype(BF16)

    @pl.when(odd == 0)
    def _():
        arrange(0, mine)
        arrange(1, theirs)

    @pl.when(odd == 1)
    def _():
        arrange(1, mine)
        arrange(0, theirs)

    sender_grad = dot(by_sender, w1[WIDTH : 2 * WIDTH], NT)
    node_grad[...] = sender_grad[:ROWS] + dot(by_receiver, w1[2 * WIDTH :], NT)
    ret_pair[...] = sender_grad[ROWS : ROWS + HALO].astype(BF16)
    ret_cross[...] = sender_grad[ROWS + HALO :].astype(BF16)


def local_grads(*args):
    shapes = (
        ((SLOTS, WIDTH), BF16),
        ((SLOTS, WIDTH), BF16),
        ((SLOTS, WIDTH), BF16),
        ((ROWS, WIDTH), F32),
        ((HALO, WIDTH), BF16),
        ((HALO, WIDTH), BF16),
    )
    vmem = pl.BlockSpec(memory_space=pltpu.VMEM)
    return pl.pallas_call(
        kernel,
        out_shape=[jax.ShapeDtypeStruct(s, d) for s, d in shapes],
        in_specs=[pl.BlockSpec(memory_space=pltpu.SMEM)] + [vmem] * 10,
        out_specs=[vmem] * 6,
        scratch_shapes=[
            pltpu.VMEM((SLOTS, WIDTH), BF16),
            pltpu.VMEM((2 * ROWS + 2 * HALO, SLOTS), BF16),
            pltpu.VMEM((ROWS + 2 * HALO, WIDTH), BF16),
            pltpu.VMEM((3 * WIDTH, WIDTH), F32),
        ],
        compiler_params=pltpu.CompilerParams(vmem_limit_bytes=48 * 1024 * 1024),
        cost_estimate=pl.CostEstimate(
            flops=6_000_000_000, bytes_accessed=8_000_000, transcendentals=400_000
        ),
    )(*args)


def exchange(block, groups):
    return lax.all_to_all(block, AXES, 0, 0, axis_index_groups=groups)


def total(block):
    return jnp.sum(block.astype(F32), axis=0)


def per_device(
    nodes, edges, d_new_edges, d_aggregate, edge_w1, edge_w2, senders, receivers, edge_count
):
    here = lax.axis_index("patch")
    odd = here % 2
    first = nodes[:HALO]
    last = nodes[ROWS - HALO :]
    pair = lax.ppermute(jnp.where(odd == 0, last, first), "patch", PAIR)
    cross = lax.ppermute(jnp.where(odd == 0, first, last), "patch", CROSS)
    scalars = jnp.stack([here, odd, edge_count[0]]).astype(jnp.int32)
    mine, theirs, edge_grad, node_grad, ret_pair, ret_cross = local_grads(
        scalars,
        senders.reshape(6, 128),
        receivers.reshape(6, 128),
        nodes,
        pair,
        cross,
        edges,
        d_new_edges,
        d_aggregate,
        edge_w1,
        edge_w2,
    )
    other = lax.ppermute(theirs, "patch", PAIR)
    from_pair = lax.ppermute(ret_pair, "patch", PAIR).astype(F32)
    from_cross = lax.ppermute(ret_cross, "patch", CROSS).astype(F32)
    weight = (mine.astype(F32) + other.astype(F32)).astype(BF16).reshape(8, 96, WIDTH)
    weight = total(exchange(weight, X_AND_Y_PAIR)).astype(BF16).reshape(4, 24, WIDTH)
    weight = total(exchange(weight, Y_QUADS)).astype(BF16)
    weight = jnp.broadcast_to(weight[None], (8, 24, WIDTH))
    weight_grad = total(exchange(weight, Z_ALL))
    from_lower = jnp.where(odd == 1, from_pair, from_cross)
    from_upper = jnp.where(odd == 1, from_cross, from_pair)
    gap = jnp.zeros((ROWS - 2 * HALO, WIDTH), F32)
    node_grad = node_grad + jnp.concatenate([from_lower, gap, from_upper], axis=0)
    return (node_grad.astype(BF16), edge_grad, weight_grad)


def solution(mesh):
    placed = (
        P(AXES, None),
        P(AXES, None),
        P(AXES, None),
        P(AXES, None),
        P(),
        P(),
        P(AXES),
        P(AXES),
        P(AXES),
    )
    return jax.shard_map(
        per_device,
        mesh=mesh,
        in_specs=placed,
        out_specs=(P(AXES, None), P(AXES, None), P("patch", None)),
        check_vma=False,
    )
```

```python
import itertools

import jax
import jax.numpy as jnp
from jax import lax
from jax.experimental import pallas as pl
from jax.experimental.pallas import tpu as pltpu
from jax.sharding import PartitionSpec as P

HALO = 32
ROWS = 128
SLOTS = 768
WIDTH = 512
PLACES = 2 * ROWS + 2 * HALO
BLOCK = 768
AXES = ("patch", "band")
BF16 = jnp.bfloat16
F32 = jnp.float32
VMEM = pl.BlockSpec(memory_space=pltpu.VMEM)
SMEM = pl.BlockSpec(memory_space=pltpu.SMEM)
HBM = pl.BlockSpec(memory_space=pl.ANY)


def device_groups(y_parts, x_parts, z_parts):
    groups = []
    for ys, xs, zs, core in itertools.product(y_parts, x_parts, z_parts, range(2)):
        groups.append(
            [((y * 4 + x) * 2 + core) * 8 + z for x, y, z in itertools.product(xs, ys, zs)]
        )
    return groups


SINGLE_X, SINGLE_Y, SINGLE_Z = ([[i] for i in range(n)] for n in (4, 8, 8))
X_AND_Y_PAIR = device_groups([[2 * i, 2 * i + 1] for i in range(4)], [list(range(4))], SINGLE_Z)
Y_QUADS = device_groups([[0, 2, 4, 6], [1, 3, 5, 7]], SINGLE_X, SINGLE_Z)
Z_ALL = device_groups(SINGLE_Y, SINGLE_X, [list(range(8))])
PAIR = [(i, i ^ 1) for i in range(64)]
CROSS = [(i, (i - 1) % 64 if i % 2 == 0 else (i + 1) % 64) for i in range(64)]

NN = ((1,), (0,))
NT = ((1,), (1,))
TN = ((0,), (0,))


def dot(a, b, dims=NN):
    return lax.dot_general(a, b, (dims, ((), ())), preferred_element_type=F32)


def hot(mask):
    return jnp.where(mask, 1.0, 0.0).astype(BF16)


def halves(values):
    high = values.astype(BF16)
    return jnp.concatenate([high, (values - high.astype(F32)).astype(BF16)], axis=0)


def prepare_kernel(
    scalars,
    senders_hbm,
    receivers_hbm,
    nodes_hbm,
    edges_hbm,
    d_new_hbm,
    d_agg_hbm,
    w1_hbm,
    w2_hbm,
    base,
    grad_new,
    edges_t,
    scatter,
    halo_hot,
    w1,
    w2,
    nodes,
    edges,
    d_new,
    d_agg,
    senders,
    receivers,
    sems,
):
    pairs = (
        (senders_hbm, senders),
        (receivers_hbm, receivers),
        (nodes_hbm, nodes),
        (w1_hbm, w1),
        (edges_hbm, edges),
        (d_agg_hbm, d_agg),
        (d_new_hbm, d_new),
        (w2_hbm, w2),
    )
    copies = [pltpu.make_async_copy(a, b, sems.at[i]) for i, (a, b) in enumerate(pairs)]
    for copy in copies:
        copy.start()
    here, odd, count = scalars[0], scalars[1], scalars[2]
    copies[0].wait()
    copies[1].wait()
    owner = senders[...] // (ROWS * 8)
    offset = senders[...] % ROWS
    lower = jnp.where(here == 0, 63, here - 1)
    lower_base = jnp.where(odd == 1, ROWS, ROWS + HALO) - (ROWS - HALO)
    upper_base = jnp.where(odd == 1, ROWS + HALO, ROWS)
    position = jnp.where(
        owner == here, offset, jnp.where(owner == lower, lower_base + offset, upper_base + offset)
    )
    receive = receivers[...]

    def columns(index, part):
        return jnp.broadcast_to(index[part : part + 1, :], (128, 128)).T

    lane = lax.broadcasted_iota(jnp.int32, (128, 128), 1)
    send_hot, recv_hot = [], []
    for part in range(SLOTS // 128):
        place = columns(position, part)
        send_hot.append(hot(place == lane))
        halo_hot[part * 128 : part * 128 + 128, :] = hot(place == ROWS + lane % 64)
        recv_hot.append(hot(columns(receive, part) == lane))
        row = slice(part * 128, part * 128 + 128)
        scatter[: ROWS + 2 * HALO, row] = hot(
            lax.broadcasted_iota(jnp.int32, (192, 128), 0) == position[part : part + 1, :]
        )
        scatter[ROWS + 2 * HALO :, row] = hot(
            lax.broadcasted_iota(jnp.int32, (128, 128), 0) == receive[part : part + 1, :]
        )
    copies[2].wait()
    copies[3].wait()
    product = jnp.concatenate(
        [
            halves(dot(nodes[...], w1[WIDTH : 2 * WIDTH])),
            halves(dot(nodes[...], w1[2 * WIDTH :])),
        ],
        axis=0,
    )
    copies[4].wait()
    for start in range(0, SLOTS, BLOCK):
        rows = slice(start, start + BLOCK)
        parts = range(start // 128, (start + BLOCK) // 128)
        gather = jnp.concatenate(
            [
                jnp.concatenate([send_hot[p], send_hot[p], recv_hot[p], recv_hot[p]], axis=1)
                for p in parts
            ],
            axis=0,
        )
        base[rows, :] = dot(edges[rows, :], w1[:WIDTH]) + dot(gather, product)
        edges_t[:, rows] = edges[rows, :].T
    copies[5].wait()
    copies[6].wait()
    for start in range(0, SLOTS, BLOCK):
        rows = slice(start, start + BLOCK)
        parts = range(start // 128, (start + BLOCK) // 128)
        slot = start + lax.broadcasted_iota(jnp.int32, (BLOCK, 1), 0)
        live = jnp.where(slot < count, 1.0, 0.0)
        taken = dot(jnp.concatenate([recv_hot[p] for p in parts], axis=0), d_agg[...])
        grad_new[rows, :] = live * (d_new[rows, :].astype(F32) + taken)
    copies[7].wait()


def prepare(*args):
    shapes = (
        ((SLOTS, WIDTH), F32),
        ((SLOTS, WIDTH), F32),
        ((WIDTH, SLOTS), BF16),
        ((PLACES, SLOTS), BF16),
        ((SLOTS, 128), BF16),
        ((3 * WIDTH, WIDTH), BF16),
        ((WIDTH, WIDTH), BF16),
        ((ROWS, WIDTH), BF16),
    )
    args = args[:1] + tuple(pltpu.with_memory_space_constraint(a, pltpu.HBM) for a in args[1:])
    return pl.pallas_call(
        prepare_kernel,
        out_shape=[pltpu.VMEM(s, d) for s, d in shapes],
        in_specs=[SMEM] + [HBM] * 8,
        out_specs=[VMEM] * 8,
        scratch_shapes=[
            pltpu.VMEM((SLOTS, WIDTH), BF16),
            pltpu.VMEM((SLOTS, WIDTH), BF16),
            pltpu.VMEM((ROWS, WIDTH), BF16),
            pltpu.VMEM((6, 128), jnp.int32),
            pltpu.VMEM((6, 128), jnp.int32),
            pltpu.SemaphoreType.DMA((8,)),
        ],
        compiler_params=pltpu.CompilerParams(vmem_limit_bytes=20 * 1024 * 1024),
        cost_estimate=pl.CostEstimate(
            flops=2_000_000_000, bytes_accessed=10_000_000, transcendentals=0
        ),
    )(*args)


def weight_kernel(
    scalars,
    pair,
    cross,
    base,
    grad_new,
    edges_t,
    scatter,
    halo_hot,
    w1,
    w2,
    nodes,
    mine,
    theirs,
    dz_all,
    summed,
    ret_cross,
    weight,
):
    odd = scalars[1]
    halo = jnp.concatenate([pair[...], cross[...]], axis=0)
    halo_product = halves(dot(halo, w1[WIDTH : 2 * WIDTH]))
    for start in range(0, SLOTS, BLOCK):
        rows = slice(start, start + BLOCK)
        pre = base[rows, :] + dot(halo_hot[rows, :], halo_product)
        sigma = 0.5 * jnp.tanh(0.5 * pre) + 0.5
        hidden = pre * sigma
        out = dot(hidden.astype(BF16), w2[...])
        center = out - jnp.mean(out, axis=-1, keepdims=True)
        rstd = lax.rsqrt(jnp.mean(center * center, axis=-1, keepdims=True) + 1e-05)
        normed = center * rstd
        grad = grad_new[rows, :]
        g_out = (
            grad
            - jnp.mean(grad, axis=-1, keepdims=True)
            - normed * jnp.mean(grad * normed, axis=-1, keepdims=True)
        ) * rstd
        g_hidden = dot(g_out.astype(BF16), w2[...], NT)
        dz_all[rows, :] = (g_hidden * (sigma + hidden * (1.0 - sigma))).astype(BF16)
    dz = dz_all[...]
    by_place = dot(scatter[...], dz).astype(BF16)
    summed[...] = by_place
    returned = dot(by_place[ROWS : ROWS + 2 * HALO], w1[WIDTH : 2 * WIDTH], NT).astype(BF16)
    theirs[SLOTS:, :] = returned[:HALO]
    ret_cross[...] = returned[HALO:]
    table = jnp.concatenate([nodes[...], halo], axis=0)
    weight[:WIDTH] = dot(edges_t[...], dz)
    weight[WIDTH : 2 * WIDTH] = dot(table, by_place[: ROWS + 2 * HALO], TN)
    weight[2 * WIDTH :] = dot(nodes[...], by_place[ROWS + 2 * HALO :], TN)
    for target, core in ((mine, odd), (theirs, 1 - odd)):
        for x, y in itertools.product(range(4), range(2)):
            pieces = []
            for quad in range(4):
                first = ((quad * 2 + y) * 4 + x) * 48 + core * 24
                pieces.append(weight[pl.ds(pl.multiple_of(first, 8), 24), :])
            place = (x * 2 + y) * 96
            target[place : place + 96, :] = jnp.concatenate(pieces, axis=0).astype(BF16)


def weight_terms(*args):
    shapes = (
        ((SLOTS, WIDTH), BF16),
        ((SLOTS + HALO, WIDTH), BF16),
        ((SLOTS, WIDTH), BF16),
        ((PLACES, WIDTH), BF16),
        ((HALO, WIDTH), BF16),
    )
    return pl.pallas_call(
        weight_kernel,
        out_shape=[pltpu.VMEM(s, d) for s, d in shapes],
        in_specs=[SMEM] + [VMEM] * 10,
        out_specs=[VMEM] * 5,
        scratch_shapes=[pltpu.VMEM((3 * WIDTH, WIDTH), F32)],
        compiler_params=pltpu.CompilerParams(vmem_limit_bytes=20 * 1024 * 1024),
        cost_estimate=pl.CostEstimate(
            flops=2_000_000_000, bytes_accessed=10_000_000, transcendentals=400_000
        ),
    )(*args)


def finish_kernel(grad_new, summed, dz, w1, d_edges, node_grad):
    node_grad[...] = dot(summed[:ROWS], w1[WIDTH : 2 * WIDTH], NT) + dot(
        summed[ROWS + 2 * HALO :], w1[2 * WIDTH :], NT
    )
    d_edges[...] = (grad_new[...] + dot(dz[...], w1[:WIDTH], NT)).astype(BF16)


def finish(*args):
    return pl.pallas_call(
        finish_kernel,
        out_shape=[
            jax.ShapeDtypeStruct((SLOTS, WIDTH), BF16),
            jax.ShapeDtypeStruct((ROWS, WIDTH), F32),
        ],
        in_specs=[VMEM] * 4,
        out_specs=[VMEM] * 2,
        compiler_params=pltpu.CompilerParams(vmem_limit_bytes=20 * 1024 * 1024),
        cost_estimate=pl.CostEstimate(
            flops=1_000_000_000, bytes_accessed=5_000_000, transcendentals=0
        ),
    )(*args)


def exchange(block, groups):
    return lax.all_to_all(block, AXES, 0, 0, axis_index_groups=groups)


def add_kernel(mine, other, result):
    result[...] = (mine[...].astype(F32) + other[:SLOTS].astype(F32)).astype(BF16)


def add(mine, other):
    return pl.pallas_call(
        add_kernel,
        out_shape=pltpu.VMEM((SLOTS, WIDTH), BF16),
        in_specs=[VMEM] * 2,
        out_specs=VMEM,
        compiler_params=pltpu.CompilerParams(vmem_limit_bytes=8 * 1024 * 1024),
    )(mine, other)


def sum_kernel(terms, result):
    values = jnp.sum(terms[...].astype(F32), axis=0).astype(result.dtype)
    if len(result.shape) == 2:
        result[...] = values
    else:
        for copy in range(result.shape[0]):
            result[copy] = values


def total(terms, dtype, copies=None):
    shape = terms.shape[1:] if copies is None else (copies,) + terms.shape[1:]
    return pl.pallas_call(
        sum_kernel,
        out_shape=pltpu.VMEM(shape, dtype) if dtype == BF16 else jax.ShapeDtypeStruct(shape, dtype),
        in_specs=[VMEM],
        out_specs=VMEM,
        compiler_params=pltpu.CompilerParams(vmem_limit_bytes=8 * 1024 * 1024),
    )(terms)


def per_device(
    nodes, edges, d_new_edges, d_aggregate, edge_w1, edge_w2, senders, receivers, edge_count
):
    here = lax.axis_index("patch")
    odd = here % 2
    first = nodes[:HALO]
    last = nodes[ROWS - HALO :]
    pair = lax.ppermute(jnp.where(odd == 0, last, first), "patch", PAIR)
    cross = lax.ppermute(jnp.where(odd == 0, first, last), "patch", CROSS)
    scalars = jnp.stack([here, odd, edge_count[0]]).astype(jnp.int32)
    base, grad_new, edges_t, scatter, halo_hot, w1, w2, own = prepare(
        scalars,
        senders.reshape(6, 128),
        receivers.reshape(6, 128),
        nodes,
        edges,
        d_new_edges,
        d_aggregate,
        edge_w1,
        edge_w2,
    )
    mine, theirs, dz, summed, ret_cross = weight_terms(
        scalars, pair, cross, base, grad_new, edges_t, scatter, halo_hot, w1, w2, own
    )
    other = lax.ppermute(theirs, "patch", PAIR)
    edge_grad, node_grad = finish(grad_new, summed, dz, w1)
    other, node_grad, ret_cross = lax.optimization_barrier((other, node_grad, ret_cross))
    from_pair = other[SLOTS:].astype(F32)
    from_cross = lax.ppermute(ret_cross, "patch", CROSS)
    weight = add(mine, other).reshape(8, 96, WIDTH)
    weight = total(exchange(weight, X_AND_Y_PAIR), BF16).reshape(4, 24, WIDTH)
    weight, from_cross = lax.optimization_barrier((weight, from_cross))
    from_cross = from_cross.astype(F32)
    weight = total(exchange(weight, Y_QUADS), BF16, 8)
    weight_grad = total(exchange(weight, Z_ALL), F32)
    from_lower = jnp.where(odd == 1, from_pair, from_cross)
    from_upper = jnp.where(odd == 1, from_cross, from_pair)
    gap = jnp.zeros((ROWS - 2 * HALO, WIDTH), F32)
    node_grad = node_grad + jnp.concatenate([from_lower, gap, from_upper], axis=0)
    return (node_grad.astype(BF16), edge_grad, weight_grad)


def solution(mesh):
    placed = (
        P(AXES, None),
        P(AXES, None),
        P(AXES, None),
        P(AXES, None),
        P(),
        P(),
        P(AXES),
        P(AXES),
        P(AXES),
    )
    return jax.shard_map(
        per_device,
        mesh=mesh,
        in_specs=placed,
        out_specs=(P(AXES, None), P(AXES, None), P("patch", None)),
        check_vma=False,
    )
```

```python
import itertools

import jax
import jax.numpy as jnp
from jax import lax
from jax.experimental import pallas as pl
from jax.experimental.pallas import tpu as pltpu
from jax.sharding import PartitionSpec as P

HALO = 32
ROWS = 128
SLOTS = 768
WIDTH = 512
PLACES = 2 * ROWS + 2 * HALO
HALF = WIDTH // 2
BLOCK = 768
AXES = ("patch", "band")
BF16 = jnp.bfloat16
F32 = jnp.float32
VMEM = pl.BlockSpec(memory_space=pltpu.VMEM)
SMEM = pl.BlockSpec(memory_space=pltpu.SMEM)
HBM = pl.BlockSpec(memory_space=pl.ANY)


def device_groups(y_parts, x_parts, z_parts):
    groups = []
    for ys, xs, zs, core in itertools.product(y_parts, x_parts, z_parts, range(2)):
        groups.append(
            [((y * 4 + x) * 2 + core) * 8 + z for x, y, z in itertools.product(xs, ys, zs)]
        )
    return groups


PAIRS_OF_8 = [[2 * i, 2 * i + 1] for i in range(4)]
NEAR = device_groups(PAIRS_OF_8, [list(range(4))], PAIRS_OF_8)
FAR = device_groups([[0, 2, 4, 6], [1, 3, 5, 7]], [[i] for i in range(4)], [list(range(8))])
PAIR = [(i, i ^ 1) for i in range(64)]
CROSS = [(i, (i - 1) % 64 if i % 2 == 0 else (i + 1) % 64) for i in range(64)]

NN = ((1,), (0,))
NT = ((1,), (1,))
TN = ((0,), (0,))


def dot(a, b, dims=NN):
    return lax.dot_general(a, b, (dims, ((), ())), preferred_element_type=F32)


def hot(mask):
    return jnp.where(mask, 1.0, 0.0).astype(BF16)


def halves(values):
    high = values.astype(BF16)
    return jnp.concatenate([high, (values - high.astype(F32)).astype(BF16)], axis=0)


def prepare_kernel(
    count,
    senders_hbm,
    receivers_hbm,
    nodes_hbm,
    edges_hbm,
    d_new_hbm,
    d_agg_hbm,
    w1_hbm,
    w2_hbm,
    base,
    grad_new,
    edges_t,
    scatter,
    halo_hot,
    w1,
    w2,
    nodes,
    edges,
    d_new,
    d_agg,
    senders,
    receivers,
    sems,
):
    pairs = (
        (senders_hbm, senders),
        (receivers_hbm, receivers),
        (nodes_hbm, nodes),
        (w1_hbm, w1),
        (edges_hbm, edges),
        (d_agg_hbm, d_agg),
        (d_new_hbm, d_new),
        (w2_hbm, w2),
    )
    copies = [pltpu.make_async_copy(a, b, sems.at[i]) for i, (a, b) in enumerate(pairs)]
    for copy in copies:
        copy.start()
    here = lax.axis_index("patch")
    odd = here % 2
    copies[0].wait()
    copies[1].wait()
    owner = senders[...] // (ROWS * 8)
    offset = senders[...] % ROWS
    lower = jnp.where(here == 0, 63, here - 1)
    lower_base = jnp.where(odd == 1, ROWS, ROWS + HALO) - (ROWS - HALO)
    upper_base = jnp.where(odd == 1, ROWS + HALO, ROWS)
    position = jnp.where(
        owner == here, offset, jnp.where(owner == lower, lower_base + offset, upper_base + offset)
    )
    receive = receivers[...]

    def columns(index, part):
        return jnp.broadcast_to(index[part : part + 1, :], (128, 128)).T

    lane = lax.broadcasted_iota(jnp.int32, (128, 128), 1)
    send_hot, recv_hot = [], []
    for part in range(SLOTS // 128):
        place = columns(position, part)
        send_hot.append(hot(place == lane))
        halo_hot[part * 128 : part * 128 + 128, :] = hot(place == ROWS + lane % 64)
        recv_hot.append(hot(columns(receive, part) == lane))
        row = slice(part * 128, part * 128 + 128)
        scatter[: ROWS + 2 * HALO, row] = hot(
            lax.broadcasted_iota(jnp.int32, (192, 128), 0) == position[part : part + 1, :]
        )
        scatter[ROWS + 2 * HALO :, row] = hot(
            lax.broadcasted_iota(jnp.int32, (128, 128), 0) == receive[part : part + 1, :]
        )
    copies[2].wait()
    copies[3].wait()
    product = jnp.concatenate(
        [
            halves(dot(nodes[...], w1[WIDTH : 2 * WIDTH])),
            halves(dot(nodes[...], w1[2 * WIDTH :])),
        ],
        axis=0,
    )
    copies[4].wait()
    for start in range(0, SLOTS, BLOCK):
        rows = slice(start, start + BLOCK)
        parts = range(start // 128, (start + BLOCK) // 128)
        gather = jnp.concatenate(
            [
                jnp.concatenate([send_hot[p], send_hot[p], recv_hot[p], recv_hot[p]], axis=1)
                for p in parts
            ],
            axis=0,
        )
        base[rows, :] = dot(edges[rows, :], w1[:WIDTH]) + dot(gather, product)
        edges_t[:, rows] = edges[rows, :].T
    copies[5].wait()
    copies[6].wait()
    limit = jnp.broadcast_to(count[0:1, 0:1], (SLOTS, 1))
    for start in range(0, SLOTS, BLOCK):
        rows = slice(start, start + BLOCK)
        parts = range(start // 128, (start + BLOCK) // 128)
        slot = start + lax.broadcasted_iota(jnp.int32, (BLOCK, 1), 0)
        live = jnp.where(slot < limit[rows], 1.0, 0.0)
        taken = dot(jnp.concatenate([recv_hot[p] for p in parts], axis=0), d_agg[...])
        grad_new[rows, :] = live * (d_new[rows, :].astype(F32) + taken)
    copies[7].wait()


def prepare(*args):
    shapes = (
        ((SLOTS, WIDTH), F32),
        ((SLOTS, WIDTH), F32),
        ((WIDTH, SLOTS), BF16),
        ((PLACES, SLOTS), BF16),
        ((SLOTS, 128), BF16),
        ((3 * WIDTH, WIDTH), BF16),
        ((WIDTH, WIDTH), BF16),
        ((ROWS, WIDTH), BF16),
    )
    args = args[:1] + tuple(pltpu.with_memory_space_constraint(a, pltpu.HBM) for a in args[1:])
    return pl.pallas_call(
        prepare_kernel,
        out_shape=[pltpu.VMEM(s, d) for s, d in shapes],
        in_specs=[VMEM] + [HBM] * 8,
        out_specs=[VMEM] * 8,
        scratch_shapes=[
            pltpu.VMEM((SLOTS, WIDTH), BF16),
            pltpu.VMEM((SLOTS, WIDTH), BF16),
            pltpu.VMEM((ROWS, WIDTH), BF16),
            pltpu.VMEM((6, 128), jnp.int32),
            pltpu.VMEM((6, 128), jnp.int32),
            pltpu.SemaphoreType.DMA((8,)),
        ],
        compiler_params=pltpu.CompilerParams(vmem_limit_bytes=20 * 1024 * 1024),
        cost_estimate=pl.CostEstimate(
            flops=2_000_000_000, bytes_accessed=10_000_000, transcendentals=0
        ),
    )(*args)


def weight_kernel(
    cross,
    pair,
    base,
    grad_new,
    edges_t,
    scatter,
    halo_hot,
    w1,
    w2,
    nodes,
    mine,
    theirs,
    dz_all,
    summed,
    ret_cross,
    weight,
):
    odd = lax.axis_index("patch") % 2
    first = pl.multiple_of(odd * (ROWS - HALO), HALO)
    last = pl.multiple_of((1 - odd) * (ROWS - HALO), HALO)
    halo = jnp.concatenate([pair[pl.ds(first, HALO), :], cross[pl.ds(last, HALO), :]], axis=0)
    halo_product = halves(dot(halo, w1[WIDTH : 2 * WIDTH]))
    for start in range(0, SLOTS, BLOCK):
        rows = slice(start, start + BLOCK)
        pre = base[rows, :] + dot(halo_hot[rows, :], halo_product)
        sigma = 0.5 * jnp.tanh(0.5 * pre) + 0.5
        hidden = pre * sigma
        out = dot(hidden.astype(BF16), w2[...])
        center = out - jnp.mean(out, axis=-1, keepdims=True)
        rstd = lax.rsqrt(jnp.mean(center * center, axis=-1, keepdims=True) + 1e-05)
        normed = center * rstd
        grad = grad_new[rows, :]
        g_out = (
            grad
            - jnp.mean(grad, axis=-1, keepdims=True)
            - normed * jnp.mean(grad * normed, axis=-1, keepdims=True)
        ) * rstd
        g_hidden = dot(g_out.astype(BF16), w2[...], NT)
        dz_all[rows, :] = (g_hidden * (sigma + hidden * (1.0 - sigma))).astype(BF16)
    dz = dz_all[...]
    by_place = dot(scatter[...], dz).astype(BF16)
    summed[...] = by_place
    returned = dot(by_place[ROWS : ROWS + 2 * HALO], w1[WIDTH : 2 * WIDTH], NT).astype(BF16)
    theirs[2 * SLOTS : 2 * SLOTS + HALO, :] = returned[:HALO, :HALF]
    theirs[2 * SLOTS + HALO :, :] = returned[:HALO, HALF:]
    ret_cross[...] = returned[HALO:]
    table = jnp.concatenate([nodes[...], halo], axis=0)
    weight[:WIDTH] = dot(edges_t[...], dz)
    weight[WIDTH : 2 * WIDTH] = dot(table, by_place[: ROWS + 2 * HALO], TN)
    weight[2 * WIDTH :] = dot(nodes[...], by_place[ROWS + 2 * HALO :], TN)
    for target, core in ((mine, odd), (theirs, 1 - odd)):
        for x, y, z in itertools.product(range(4), range(2), range(2)):
            pieces = []
            for quad in range(4):
                first = ((quad * 2 + y) * 4 + x) * 48 + core * 24
                rows = pl.ds(pl.multiple_of(first, 8), 24)
                pieces.append(weight[rows, z * HALF : z * HALF + HALF])
            place = ((x * 2 + y) * 2 + z) * 96
            target[place : place + 96, :] = jnp.concatenate(pieces, axis=0).astype(BF16)


def weight_terms(*args):
    shapes = (
        ((2 * SLOTS, HALF), BF16),
        ((2 * SLOTS + 2 * HALO, HALF), BF16),
        ((SLOTS, WIDTH), BF16),
        ((PLACES, WIDTH), BF16),
        ((HALO, WIDTH), BF16),
    )
    return pl.pallas_call(
        weight_kernel,
        out_shape=[pltpu.VMEM(s, d) for s, d in shapes],
        in_specs=[VMEM] * 10,
        out_specs=[VMEM] * 5,
        scratch_shapes=[pltpu.VMEM((3 * WIDTH, WIDTH), F32)],
        compiler_params=pltpu.CompilerParams(vmem_limit_bytes=20 * 1024 * 1024),
        cost_estimate=pl.CostEstimate(
            flops=2_000_000_000, bytes_accessed=10_000_000, transcendentals=400_000
        ),
    )(*args)


def finish_kernel(grad_new, summed, dz, w1, d_edges, node_grad):
    node_grad[...] = dot(summed[:ROWS], w1[WIDTH : 2 * WIDTH], NT) + dot(
        summed[ROWS + 2 * HALO :], w1[2 * WIDTH :], NT
    )
    d_edges[...] = (grad_new[...] + dot(dz[...], w1[:WIDTH], NT)).astype(BF16)


def finish(*args):
    return pl.pallas_call(
        finish_kernel,
        out_shape=[
            jax.ShapeDtypeStruct((SLOTS, WIDTH), BF16),
            jax.ShapeDtypeStruct((ROWS, WIDTH), F32),
        ],
        in_specs=[VMEM] * 4,
        out_specs=[VMEM] * 2,
        compiler_params=pltpu.CompilerParams(vmem_limit_bytes=20 * 1024 * 1024),
        cost_estimate=pl.CostEstimate(
            flops=1_000_000_000, bytes_accessed=5_000_000, transcendentals=0
        ),
    )(*args)


def exchange(block, groups):
    return lax.all_to_all(block, AXES, 0, 0, axis_index_groups=groups)


def small_call(body, shape, dtype, *args):
    return pl.pallas_call(
        body,
        out_shape=pltpu.VMEM(shape, dtype) if dtype == BF16 else jax.ShapeDtypeStruct(shape, dtype),
        in_specs=[VMEM] * len(args),
        out_specs=VMEM,
        compiler_params=pltpu.CompilerParams(vmem_limit_bytes=8 * 1024 * 1024),
    )(*args)


def add_kernel(mine, other, result):
    result[...] = (mine[...].astype(F32) + other[: 2 * SLOTS].astype(F32)).astype(BF16)


def near_kernel(terms, result):
    values = jnp.sum(terms[...].astype(F32), axis=0)
    for quad in range(4):
        piece = values[quad * 24 : quad * 24 + 24].astype(BF16)
        for z in range(8):
            result[quad * 8 + z] = piece


def far_kernel(terms, result):
    for half in range(2):
        values = terms[half].astype(F32)
        for place in range(2 + half, 32, 2):
            values = values + terms[place].astype(F32)
        result[:, half * HALF : half * HALF + HALF] = values


def per_device(
    nodes, edges, d_new_edges, d_aggregate, edge_w1, edge_w2, senders, receivers, edge_count
):
    here = lax.axis_index("patch")
    odd = here % 2
    cross = lax.ppermute(nodes, "patch", CROSS)
    pair = lax.ppermute(nodes, "patch", PAIR)
    base, grad_new, edges_t, scatter, halo_hot, w1, w2, own = prepare(
        jnp.broadcast_to(edge_count, (8, 128)),
        senders.reshape(6, 128),
        receivers.reshape(6, 128),
        nodes,
        edges,
        d_new_edges,
        d_aggregate,
        edge_w1,
        edge_w2,
    )
    mine, theirs, dz, summed, ret_cross = weight_terms(
        cross, pair, base, grad_new, edges_t, scatter, halo_hot, w1, w2, own
    )
    other = lax.ppermute(theirs, "patch", PAIR)
    edge_grad, node_grad = finish(grad_new, summed, dz, w1)
    other, node_grad = lax.optimization_barrier((other, node_grad))
    from_pair = jnp.concatenate([other[2 * SLOTS : -HALO], other[-HALO:]], axis=1).astype(F32)
    weight = small_call(add_kernel, (2 * SLOTS, HALF), BF16, mine, other)
    weight = exchange(weight.reshape(16, 96, HALF), NEAR)
    weight = small_call(near_kernel, (32, 24, HALF), BF16, weight)
    weight, ret_cross = lax.optimization_barrier((weight, ret_cross))
    from_cross = lax.ppermute(ret_cross, "patch", CROSS).astype(F32)
    weight_grad = small_call(far_kernel, (24, WIDTH), F32, exchange(weight, FAR))
    from_lower = jnp.where(odd == 1, from_pair, from_cross)
    from_upper = jnp.where(odd == 1, from_cross, from_pair)
    gap = jnp.zeros((ROWS - 2 * HALO, WIDTH), F32)
    node_grad = node_grad + jnp.concatenate([from_lower, gap, from_upper], axis=0)
    return (node_grad.astype(BF16), edge_grad, weight_grad)


def solution(mesh):
    placed = (
        P(AXES, None),
        P(AXES, None),
        P(AXES, None),
        P(AXES, None),
        P(),
        P(),
        P(AXES),
        P(AXES),
        P(AXES),
    )
    return jax.shard_map(
        per_device,
        mesh=mesh,
        in_specs=placed,
        out_specs=(P(AXES, None), P(AXES, None), P("patch", None)),
        check_vma=False,
    )
```

```python
import itertools

import jax
import jax.numpy as jnp
from jax import lax
from jax.experimental import pallas as pl
from jax.experimental.pallas import tpu as pltpu
from jax.sharding import PartitionSpec as P

HALO = 32
ROWS = 128
SLOTS = 768
WIDTH = 512
PLACES = 2 * ROWS + 2 * HALO
HALF = WIDTH // 2
BLOCK = 768
AXES = ("patch", "band")
BF16 = jnp.bfloat16
F32 = jnp.float32
VMEM = pl.BlockSpec(memory_space=pltpu.VMEM)
SMEM = pl.BlockSpec(memory_space=pltpu.SMEM)
HBM = pl.BlockSpec(memory_space=pl.ANY)


def device_groups(y_parts, x_parts, z_parts):
    groups = []
    for ys, xs, zs, core in itertools.product(y_parts, x_parts, z_parts, range(2)):
        groups.append(
            [((y * 4 + x) * 2 + core) * 8 + z for x, y, z in itertools.product(xs, ys, zs)]
        )
    return groups


PAIR_ORDER = (1, 0)
QUAD_ORDER = (1, 2, 3, 0)
Z_ORDER = (7, 6, 5, 4, 3, 2, 1, 0)
PAIRS_OF_8 = [[2 * i + k for k in PAIR_ORDER] for i in range(4)]
NEAR = device_groups(PAIRS_OF_8, [list(range(4))], PAIRS_OF_8)
FAR = device_groups(
    [[2 * q + k for q in QUAD_ORDER] for k in range(2)], [[i] for i in range(4)], [Z_ORDER]
)
PAIR = [(i, i ^ 1) for i in range(64)]
CROSS = [(i, (i - 1) % 64 if i % 2 == 0 else (i + 1) % 64) for i in range(64)]

NN = ((1,), (0,))
NT = ((1,), (1,))
TN = ((0,), (0,))


def dot(a, b, dims=NN):
    return lax.dot_general(a, b, (dims, ((), ())), preferred_element_type=F32)


def hot(mask):
    return jnp.where(mask, 1.0, 0.0).astype(BF16)


def halves(values):
    high = values.astype(BF16)
    return jnp.concatenate([high, (values - high.astype(F32)).astype(BF16)], axis=0)


def lane_kernel(after, lane):
    lane[...] = lax.broadcasted_iota(jnp.int32, (128, 128), 1)


def lane_index(after):
    return pl.pallas_call(
        lane_kernel,
        out_shape=pltpu.VMEM((128, 128), jnp.int32),
        in_specs=[HBM],
        out_specs=VMEM,
        compiler_params=pltpu.CompilerParams(vmem_limit_bytes=8 * 1024 * 1024),
        cost_estimate=pl.CostEstimate(
            flops=20_000_000_000, bytes_accessed=100_000, transcendentals=0
        ),
    )(after)


def prepare_kernel(
    count,
    senders,
    receivers,
    lane_ref,
    nodes,
    edges,
    d_new,
    d_agg,
    w1,
    base,
    grad_new,
    edges_t,
    scatter,
    halo_hot,
):
    here = lax.axis_index("patch")
    odd = here % 2
    owner = senders[...] // (ROWS * 8)
    offset = senders[...] % ROWS
    lower = jnp.where(here == 0, 63, here - 1)
    lower_base = jnp.where(odd == 1, ROWS, ROWS + HALO) - (ROWS - HALO)
    upper_base = jnp.where(odd == 1, ROWS + HALO, ROWS)
    position = jnp.where(
        owner == here, offset, jnp.where(owner == lower, lower_base + offset, upper_base + offset)
    )
    receive = receivers[...]

    def columns(index, part):
        return jnp.broadcast_to(index[part : part + 1, :], (128, 128)).T

    lane = lane_ref[...]
    send_hot, recv_hot = [], []
    for part in range(SLOTS // 128):
        place = columns(position, part)
        send_hot.append(hot(place == lane))
        halo_hot[part * 128 : part * 128 + 128, :] = hot(place == ROWS + lane % 64)
        recv_hot.append(hot(columns(receive, part) == lane))
        row = slice(part * 128, part * 128 + 128)
        scatter[: ROWS + 2 * HALO, row] = hot(
            lax.broadcasted_iota(jnp.int32, (192, 128), 0) == position[part : part + 1, :]
        )
        scatter[ROWS + 2 * HALO :, row] = hot(
            lax.broadcasted_iota(jnp.int32, (128, 128), 0) == receive[part : part + 1, :]
        )
    product = jnp.concatenate(
        [
            halves(dot(nodes[...], w1[WIDTH : 2 * WIDTH])),
            halves(dot(nodes[...], w1[2 * WIDTH :])),
        ],
        axis=0,
    )
    for start in range(0, SLOTS, BLOCK):
        rows = slice(start, start + BLOCK)
        parts = range(start // 128, (start + BLOCK) // 128)
        gather = jnp.concatenate(
            [
                jnp.concatenate([send_hot[p], send_hot[p], recv_hot[p], recv_hot[p]], axis=1)
                for p in parts
            ],
            axis=0,
        )
        base[rows, :] = dot(edges[rows, :], w1[:WIDTH]) + dot(gather, product)
        edges_t[:, rows] = edges[rows, :].T
    limit = jnp.broadcast_to(count[0:1, 0:1], (SLOTS, 1))
    for start in range(0, SLOTS, BLOCK):
        rows = slice(start, start + BLOCK)
        parts = range(start // 128, (start + BLOCK) // 128)
        slot = start + lax.broadcasted_iota(jnp.int32, (BLOCK, 1), 0)
        live = jnp.where(slot < limit[rows], 1.0, 0.0)
        taken = dot(jnp.concatenate([recv_hot[p] for p in parts], axis=0), d_agg[...])
        grad_new[rows, :] = live * (d_new[rows, :].astype(F32) + taken)


def prepare(*args):
    shapes = (
        ((SLOTS, WIDTH), F32),
        ((SLOTS, WIDTH), F32),
        ((WIDTH, SLOTS), BF16),
        ((PLACES, SLOTS), BF16),
        ((SLOTS, 128), BF16),
    )
    return pl.pallas_call(
        prepare_kernel,
        out_shape=[pltpu.VMEM(s, d) for s, d in shapes],
        in_specs=[VMEM] * 9,
        out_specs=[VMEM] * 5,
        compiler_params=pltpu.CompilerParams(vmem_limit_bytes=16 * 1024 * 1024),
        cost_estimate=pl.CostEstimate(
            flops=2_000_000_000, bytes_accessed=10_000_000, transcendentals=0
        ),
    )(*args)


def weight_kernel(
    cross,
    pair,
    base,
    grad_new,
    edges_t,
    scatter,
    halo_hot,
    w1,
    w2,
    nodes,
    mine,
    theirs,
    dz_all,
    summed,
    ret_cross,
    weight,
):
    odd = lax.axis_index("patch") % 2
    halo = jnp.concatenate([pair[...], cross[...]], axis=0)
    halo_product = halves(dot(halo, w1[WIDTH : 2 * WIDTH]))
    for start in range(0, SLOTS, BLOCK):
        rows = slice(start, start + BLOCK)
        pre = base[rows, :] + dot(halo_hot[rows, :], halo_product)
        sigma = 0.5 * jnp.tanh(0.5 * pre) + 0.5
        hidden = pre * sigma
        out = dot(hidden.astype(BF16), w2[...])
        center = out - jnp.mean(out, axis=-1, keepdims=True)
        rstd = lax.rsqrt(jnp.mean(center * center, axis=-1, keepdims=True) + 1e-05)
        normed = center * rstd
        grad = grad_new[rows, :]
        g_out = (
            grad
            - jnp.mean(grad, axis=-1, keepdims=True)
            - normed * jnp.mean(grad * normed, axis=-1, keepdims=True)
        ) * rstd
        g_hidden = dot(g_out.astype(BF16), w2[...], NT)
        dz_all[rows, :] = (g_hidden * (sigma + hidden * (1.0 - sigma))).astype(BF16)
    dz = dz_all[...]
    by_place = dot(scatter[...], dz).astype(BF16)
    summed[...] = by_place
    returned = dot(by_place[ROWS : ROWS + 2 * HALO], w1[WIDTH : 2 * WIDTH], NT).astype(BF16)
    theirs[2 * SLOTS : 2 * SLOTS + HALO, :] = returned[:HALO, :HALF]
    theirs[2 * SLOTS + HALO :, :] = returned[:HALO, HALF:]
    ret_cross[...] = returned[HALO:]
    table = jnp.concatenate([nodes[...], halo], axis=0)
    weight[:WIDTH] = dot(edges_t[...], dz)
    weight[WIDTH : 2 * WIDTH] = dot(table, by_place[: ROWS + 2 * HALO], TN)
    weight[2 * WIDTH :] = dot(nodes[...], by_place[ROWS + 2 * HALO :], TN)
    for target, core in ((mine, odd), (theirs, 1 - odd)):
        for x, y, z in itertools.product(range(4), range(2), range(2)):
            pieces = []
            for quad in range(4):
                first = ((quad * 2 + y) * 4 + x) * 48 + core * 24
                rows = pl.ds(pl.multiple_of(first, 8), 24)
                pieces.append(weight[rows, z * HALF : z * HALF + HALF])
            place = ((x * 2 + PAIR_ORDER.index(y)) * 2 + PAIR_ORDER.index(z)) * 96
            target[place : place + 96, :] = jnp.concatenate(pieces, axis=0).astype(BF16)


def weight_terms(*args):
    shapes = (
        ((2 * SLOTS, HALF), BF16),
        ((2 * SLOTS + 2 * HALO, HALF), BF16),
        ((SLOTS, WIDTH), BF16),
        ((PLACES, WIDTH), BF16),
        ((HALO, WIDTH), BF16),
    )
    return pl.pallas_call(
        weight_kernel,
        out_shape=[pltpu.VMEM(s, d) for s, d in shapes],
        in_specs=[VMEM] * 10,
        out_specs=[VMEM] * 5,
        scratch_shapes=[pltpu.VMEM((3 * WIDTH, WIDTH), F32)],
        compiler_params=pltpu.CompilerParams(vmem_limit_bytes=20 * 1024 * 1024),
        cost_estimate=pl.CostEstimate(
            flops=2_000_000_000, bytes_accessed=10_000_000, transcendentals=400_000
        ),
    )(*args)


def finish_kernel(grad_new, summed, dz, w1, d_edges, node_grad):
    node_grad[...] = dot(summed[:ROWS], w1[WIDTH : 2 * WIDTH], NT) + dot(
        summed[ROWS + 2 * HALO :], w1[2 * WIDTH :], NT
    )
    d_edges[...] = (grad_new[...] + dot(dz[...], w1[:WIDTH], NT)).astype(BF16)


def finish(*args):
    return pl.pallas_call(
        finish_kernel,
        out_shape=[
            jax.ShapeDtypeStruct((SLOTS, WIDTH), BF16),
            jax.ShapeDtypeStruct((ROWS, WIDTH), F32),
        ],
        in_specs=[VMEM] * 4,
        out_specs=[VMEM] * 2,
        compiler_params=pltpu.CompilerParams(vmem_limit_bytes=20 * 1024 * 1024),
        cost_estimate=pl.CostEstimate(
            flops=1_000_000_000, bytes_accessed=5_000_000, transcendentals=0
        ),
    )(*args)


def exchange(block, groups):
    return lax.all_to_all(block, AXES, 0, 0, axis_index_groups=groups)


def small_call(body, shape, dtype, *args):
    return pl.pallas_call(
        body,
        out_shape=pltpu.VMEM(shape, dtype) if dtype == BF16 else jax.ShapeDtypeStruct(shape, dtype),
        in_specs=[VMEM] * len(args),
        out_specs=VMEM,
        compiler_params=pltpu.CompilerParams(vmem_limit_bytes=8 * 1024 * 1024),
    )(*args)


def add_kernel(mine, other, result):
    result[...] = (mine[...].astype(F32) + other[: 2 * SLOTS].astype(F32)).astype(BF16)


def near_kernel(terms, result):
    values = jnp.sum(terms[...].astype(F32), axis=0)
    for place, quad in enumerate(QUAD_ORDER):
        piece = values[quad * 24 : quad * 24 + 24].astype(BF16)
        for z in range(8):
            result[place * 8 + z] = piece


def far_kernel(terms, result):
    for half in range(2):
        places = [i for i in range(32) if Z_ORDER[i % 8] % 2 == half]
        values = terms[places[0]].astype(F32)
        for place in places[1:]:
            values = values + terms[place].astype(F32)
        result[:, half * HALF : half * HALF + HALF] = values


def per_device(
    nodes, edges, d_new_edges, d_aggregate, edge_w1, edge_w2, senders, receivers, edge_count
):
    here = lax.axis_index("patch")
    odd = here % 2
    odd = lax.axis_index("patch") % 2
    first, last = nodes[:HALO], nodes[ROWS - HALO :]
    to_cross = jnp.where(odd == 0, first, last)
    to_pair = jnp.where(odd == 0, last, first)
    lane, to_cross, to_pair = lax.optimization_barrier((lane_index(to_cross), to_cross, to_pair))
    cross = lax.ppermute(to_cross, "patch", CROSS)
    pair = lax.ppermute(to_pair, "patch", PAIR)
    base, grad_new, edges_t, scatter, halo_hot = prepare(
        jnp.broadcast_to(edge_count, (8, 128)),
        senders.reshape(6, 128),
        receivers.reshape(6, 128),
        lane,
        nodes,
        edges,
        d_new_edges,
        d_aggregate,
        edge_w1,
    )
    mine, theirs, dz, summed, ret_cross = weight_terms(
        cross, pair, base, grad_new, edges_t, scatter, halo_hot, edge_w1, edge_w2, nodes
    )
    other = lax.ppermute(theirs, "patch", PAIR)
    edge_grad, node_grad = finish(grad_new, summed, dz, edge_w1)
    other, node_grad = lax.optimization_barrier((other, node_grad))
    from_pair = jnp.concatenate([other[2 * SLOTS : -HALO], other[-HALO:]], axis=1).astype(F32)
    weight = small_call(add_kernel, (2 * SLOTS, HALF), BF16, mine, other)
    weight = exchange(weight.reshape(16, 96, HALF), NEAR)
    weight = small_call(near_kernel, (32, 24, HALF), BF16, weight)
    weight, ret_cross = lax.optimization_barrier((weight, ret_cross))
    from_cross = lax.ppermute(ret_cross, "patch", CROSS).astype(F32)
    weight_grad = small_call(far_kernel, (24, WIDTH), F32, exchange(weight, FAR))
    from_lower = jnp.where(odd == 1, from_pair, from_cross)
    from_upper = jnp.where(odd == 1, from_cross, from_pair)
    gap = jnp.zeros((ROWS - 2 * HALO, WIDTH), F32)
    node_grad = node_grad + jnp.concatenate([from_lower, gap, from_upper], axis=0)
    return (node_grad.astype(BF16), edge_grad, weight_grad)


def solution(mesh):
    placed = (
        P(AXES, None),
        P(AXES, None),
        P(AXES, None),
        P(AXES, None),
        P(),
        P(),
        P(AXES),
        P(AXES),
        P(AXES),
    )
    return jax.shard_map(
        per_device,
        mesh=mesh,
        in_specs=placed,
        out_specs=(P(AXES, None), P(AXES, None), P("patch", None)),
        check_vma=False,
    )
```

```python
import itertools

import jax
import jax.numpy as jnp
from jax import lax
from jax.experimental import pallas as pl
from jax.experimental.pallas import tpu as pltpu
from jax.sharding import PartitionSpec as P

HALO = 32
ROWS = 128
SLOTS = 768
WIDTH = 512
PLACES = 2 * ROWS + 2 * HALO
HALF = WIDTH // 2
BLOCK = 768
AXES = ("patch", "band")
BF16 = jnp.bfloat16
F32 = jnp.float32
VMEM = pl.BlockSpec(memory_space=pltpu.VMEM)
SMEM = pl.BlockSpec(memory_space=pltpu.SMEM)
HBM = pl.BlockSpec(memory_space=pl.ANY)


def device_groups(y_parts, x_parts, z_parts):
    groups = []
    for ys, xs, zs, core in itertools.product(y_parts, x_parts, z_parts, range(2)):
        groups.append(
            [((y * 4 + x) * 2 + core) * 8 + z for x, y, z in itertools.product(xs, ys, zs)]
        )
    return groups


Y_ORDER = (0,1)
ZP_ORDER = (1,0)
X_ORDER = (2,3,0,1)
QUAD_ORDER = (1,2,3,0)
Z_ORDER = (7,6,5,4,3,2,1,0)
NEAR = device_groups([[2 * i + k for k in Y_ORDER] for i in range(4)], [X_ORDER], [[2 * i + k for k in ZP_ORDER] for i in range(4)])
FAR = device_groups(
    [[2 * q + k for q in QUAD_ORDER] for k in range(2)], [[i] for i in range(4)], [Z_ORDER]
)
PAIR = [(i, i ^ 1) for i in range(64)]
CROSS = [(i, (i - 1) % 64 if i % 2 == 0 else (i + 1) % 64) for i in range(64)]

NN = ((1,), (0,))
NT = ((1,), (1,))
TN = ((0,), (0,))


def dot(a, b, dims=NN):
    return lax.dot_general(a, b, (dims, ((), ())), preferred_element_type=F32)


def hot(mask):
    return jnp.where(mask, 1.0, 0.0).astype(BF16)


def halves(values):
    high = values.astype(BF16)
    return jnp.concatenate([high, (values - high.astype(F32)).astype(BF16)], axis=0)


def lane_kernel(after, lane):
    lane[...] = lax.broadcasted_iota(jnp.int32, (128, 128), 1)


def lane_index(after):
    return pl.pallas_call(
        lane_kernel,
        out_shape=pltpu.VMEM((128, 128), jnp.int32),
        in_specs=[HBM],
        out_specs=VMEM,
        compiler_params=pltpu.CompilerParams(vmem_limit_bytes=8 * 1024 * 1024),
        cost_estimate=pl.CostEstimate(
            flops=20_000_000_000, bytes_accessed=100_000, transcendentals=0
        ),
    )(after)


def prepare_kernel(
    count,
    senders,
    receivers,
    lane_ref,
    nodes,
    edges,
    d_new,
    d_agg,
    w1,
    base,
    grad_new,
    edges_t,
    scatter,
    halo_hot,
):
    here = lax.axis_index("patch")
    odd = here % 2
    owner = senders[...] // (ROWS * 8)
    offset = senders[...] % ROWS
    lower = jnp.where(here == 0, 63, here - 1)
    lower_base = jnp.where(odd == 1, ROWS, ROWS + HALO) - (ROWS - HALO)
    upper_base = jnp.where(odd == 1, ROWS + HALO, ROWS)
    position = jnp.where(
        owner == here, offset, jnp.where(owner == lower, lower_base + offset, upper_base + offset)
    )
    receive = receivers[...]

    def columns(index, part):
        return jnp.broadcast_to(index[part : part + 1, :], (128, 128)).T

    lane = lane_ref[...]
    send_hot, recv_hot = [], []
    for part in range(SLOTS // 128):
        place = columns(position, part)
        send_hot.append(hot(place == lane))
        halo_hot[part * 128 : part * 128 + 128, :] = hot(place == ROWS + lane % 64)
        recv_hot.append(hot(columns(receive, part) == lane))
        row = slice(part * 128, part * 128 + 128)
        scatter[: ROWS + 2 * HALO, row] = hot(
            lax.broadcasted_iota(jnp.int32, (192, 128), 0) == position[part : part + 1, :]
        )
        scatter[ROWS + 2 * HALO :, row] = hot(
            lax.broadcasted_iota(jnp.int32, (128, 128), 0) == receive[part : part + 1, :]
        )
    product = jnp.concatenate(
        [
            halves(dot(nodes[...], w1[WIDTH : 2 * WIDTH])),
            halves(dot(nodes[...], w1[2 * WIDTH :])),
        ],
        axis=0,
    )
    for start in range(0, SLOTS, BLOCK):
        rows = slice(start, start + BLOCK)
        parts = range(start // 128, (start + BLOCK) // 128)
        gather = jnp.concatenate(
            [
                jnp.concatenate([send_hot[p], send_hot[p], recv_hot[p], recv_hot[p]], axis=1)
                for p in parts
            ],
            axis=0,
        )
        base[rows, :] = dot(edges[rows, :], w1[:WIDTH]) + dot(gather, product)
        edges_t[:, rows] = edges[rows, :].T
    limit = jnp.broadcast_to(count[0:1, 0:1], (SLOTS, 1))
    for start in range(0, SLOTS, BLOCK):
        rows = slice(start, start + BLOCK)
        parts = range(start // 128, (start + BLOCK) // 128)
        slot = start + lax.broadcasted_iota(jnp.int32, (BLOCK, 1), 0)
        live = jnp.where(slot < limit[rows], 1.0, 0.0)
        taken = dot(jnp.concatenate([recv_hot[p] for p in parts], axis=0), d_agg[...])
        grad_new[rows, :] = live * (d_new[rows, :].astype(F32) + taken)


def prepare(*args):
    shapes = (
        ((SLOTS, WIDTH), F32),
        ((SLOTS, WIDTH), F32),
        ((WIDTH, SLOTS), BF16),
        ((PLACES, SLOTS), BF16),
        ((SLOTS, 128), BF16),
    )
    return pl.pallas_call(
        prepare_kernel,
        out_shape=[pltpu.VMEM(s, d) for s, d in shapes],
        in_specs=[VMEM] * 9,
        out_specs=[VMEM] * 5,
        compiler_params=pltpu.CompilerParams(vmem_limit_bytes=16 * 1024 * 1024),
        cost_estimate=pl.CostEstimate(
            flops=2_000_000_000, bytes_accessed=10_000_000, transcendentals=0
        ),
    )(*args)


def weight_kernel(
    cross,
    pair,
    base,
    grad_new,
    edges_t,
    scatter,
    halo_hot,
    w1,
    w2,
    nodes,
    mine,
    theirs,
    dz_all,
    summed,
    ret_cross,
    weight,
):
    odd = lax.axis_index("patch") % 2
    halo = jnp.concatenate([pair[...], cross[...]], axis=0)
    halo_product = halves(dot(halo, w1[WIDTH : 2 * WIDTH]))
    for start in range(0, SLOTS, BLOCK):
        rows = slice(start, start + BLOCK)
        pre = base[rows, :] + dot(halo_hot[rows, :], halo_product)
        sigma = 0.5 * jnp.tanh(0.5 * pre) + 0.5
        hidden = pre * sigma
        out = dot(hidden.astype(BF16), w2[...])
        center = out - jnp.mean(out, axis=-1, keepdims=True)
        rstd = lax.rsqrt(jnp.mean(center * center, axis=-1, keepdims=True) + 1e-05)
        normed = center * rstd
        grad = grad_new[rows, :]
        g_out = (
            grad
            - jnp.mean(grad, axis=-1, keepdims=True)
            - normed * jnp.mean(grad * normed, axis=-1, keepdims=True)
        ) * rstd
        g_hidden = dot(g_out.astype(BF16), w2[...], NT)
        dz_all[rows, :] = (g_hidden * (sigma + hidden * (1.0 - sigma))).astype(BF16)
    dz = dz_all[...]
    by_place = dot(scatter[...], dz).astype(BF16)
    summed[...] = by_place
    returned = dot(by_place[ROWS : ROWS + 2 * HALO], w1[WIDTH : 2 * WIDTH], NT).astype(BF16)
    theirs[2 * SLOTS : 2 * SLOTS + HALO, :] = returned[:HALO, :HALF]
    theirs[2 * SLOTS + HALO :, :] = returned[:HALO, HALF:]
    ret_cross[...] = returned[HALO:]
    table = jnp.concatenate([nodes[...], halo], axis=0)
    weight[:WIDTH] = dot(edges_t[...], dz)
    weight[WIDTH : 2 * WIDTH] = dot(table, by_place[: ROWS + 2 * HALO], TN)
    weight[2 * WIDTH :] = dot(nodes[...], by_place[ROWS + 2 * HALO :], TN)
    for target, core in ((mine, odd), (theirs, 1 - odd)):
        for x, y, z in itertools.product(range(4), range(2), range(2)):
            pieces = []
            for quad in range(4):
                first = ((quad * 2 + y) * 4 + x) * 48 + core * 24
                rows = pl.ds(pl.multiple_of(first, 8), 24)
                pieces.append(weight[rows, z * HALF : z * HALF + HALF])
            place = ((X_ORDER.index(x) * 2 + Y_ORDER.index(y)) * 2 + ZP_ORDER.index(z)) * 96
            target[place : place + 96, :] = jnp.concatenate(pieces, axis=0).astype(BF16)


def weight_terms(*args):
    shapes = (
        ((2 * SLOTS, HALF), BF16),
        ((2 * SLOTS + 2 * HALO, HALF), BF16),
        ((SLOTS, WIDTH), BF16),
        ((PLACES, WIDTH), BF16),
        ((HALO, WIDTH), BF16),
    )
    return pl.pallas_call(
        weight_kernel,
        out_shape=[pltpu.VMEM(s, d) for s, d in shapes],
        in_specs=[VMEM] * 10,
        out_specs=[VMEM] * 5,
        scratch_shapes=[pltpu.VMEM((3 * WIDTH, WIDTH), F32)],
        compiler_params=pltpu.CompilerParams(vmem_limit_bytes=20 * 1024 * 1024),
        cost_estimate=pl.CostEstimate(
            flops=2_000_000_000, bytes_accessed=10_000_000, transcendentals=400_000
        ),
    )(*args)


def finish_kernel(grad_new, summed, dz, w1, d_edges, node_grad):
    node_grad[...] = dot(summed[:ROWS], w1[WIDTH : 2 * WIDTH], NT) + dot(
        summed[ROWS + 2 * HALO :], w1[2 * WIDTH :], NT
    )
    d_edges[...] = (grad_new[...] + dot(dz[...], w1[:WIDTH], NT)).astype(BF16)


def finish(*args):
    return pl.pallas_call(
        finish_kernel,
        out_shape=[
            jax.ShapeDtypeStruct((SLOTS, WIDTH), BF16),
            jax.ShapeDtypeStruct((ROWS, WIDTH), F32),
        ],
        in_specs=[VMEM] * 4,
        out_specs=[VMEM] * 2,
        compiler_params=pltpu.CompilerParams(vmem_limit_bytes=20 * 1024 * 1024),
        cost_estimate=pl.CostEstimate(
            flops=1_000_000_000, bytes_accessed=5_000_000, transcendentals=0
        ),
    )(*args)


def exchange(block, groups):
    return lax.all_to_all(block, AXES, 0, 0, axis_index_groups=groups)


def small_call(body, shape, dtype, *args):
    return pl.pallas_call(
        body,
        out_shape=pltpu.VMEM(shape, dtype) if dtype == BF16 else jax.ShapeDtypeStruct(shape, dtype),
        in_specs=[VMEM] * len(args),
        out_specs=VMEM,
        compiler_params=pltpu.CompilerParams(vmem_limit_bytes=8 * 1024 * 1024),
    )(*args)


def add_kernel(mine, other, result):
    result[...] = (mine[...].astype(F32) + other[: 2 * SLOTS].astype(F32)).astype(BF16)


def near_kernel(terms, result):
    values = jnp.sum(terms[...].astype(F32), axis=0)
    for place, quad in enumerate(QUAD_ORDER):
        piece = values[quad * 24 : quad * 24 + 24].astype(BF16)
        for z in range(8):
            result[place * 8 + z] = piece


def far_kernel(terms, result):
    for half in range(2):
        places = [i for i in range(32) if Z_ORDER[i % 8] % 2 == half]
        values = terms[places[0]].astype(F32)
        for place in places[1:]:
            values = values + terms[place].astype(F32)
        result[:, half * HALF : half * HALF + HALF] = values


def per_device(
    nodes, edges, d_new_edges, d_aggregate, edge_w1, edge_w2, senders, receivers, edge_count
):
    here = lax.axis_index("patch")
    odd = here % 2
    odd = lax.axis_index("patch") % 2
    first, last = nodes[:HALO], nodes[ROWS - HALO :]
    to_cross = jnp.where(odd == 0, first, last)
    to_pair = jnp.where(odd == 0, last, first)
    lane, to_cross, to_pair = lax.optimization_barrier((lane_index(to_cross), to_cross, to_pair))
    cross = lax.ppermute(to_cross, "patch", CROSS)
    pair = lax.ppermute(to_pair, "patch", PAIR)
    base, grad_new, edges_t, scatter, halo_hot = prepare(
        jnp.broadcast_to(edge_count, (8, 128)),
        senders.reshape(6, 128),
        receivers.reshape(6, 128),
        lane,
        nodes,
        edges,
        d_new_edges,
        d_aggregate,
        edge_w1,
    )
    mine, theirs, dz, summed, ret_cross = weight_terms(
        cross, pair, base, grad_new, edges_t, scatter, halo_hot, edge_w1, edge_w2, nodes
    )
    other = lax.ppermute(theirs, "patch", PAIR)
    edge_grad, node_grad = finish(grad_new, summed, dz, edge_w1)
    other, node_grad = lax.optimization_barrier((other, node_grad))
    from_pair = jnp.concatenate([other[2 * SLOTS : -HALO], other[-HALO:]], axis=1).astype(F32)
    weight = small_call(add_kernel, (2 * SLOTS, HALF), BF16, mine, other)
    weight = exchange(weight.reshape(16, 96, HALF), NEAR)
    weight = small_call(near_kernel, (32, 24, HALF), BF16, weight)
    weight, ret_cross = lax.optimization_barrier((weight, ret_cross))
    from_cross = lax.ppermute(ret_cross, "patch", CROSS).astype(F32)
    weight_grad = small_call(far_kernel, (24, WIDTH), F32, exchange(weight, FAR))
    from_lower = jnp.where(odd == 1, from_pair, from_cross)
    from_upper = jnp.where(odd == 1, from_cross, from_pair)
    gap = jnp.zeros((ROWS - 2 * HALO, WIDTH), F32)
    node_grad = node_grad + jnp.concatenate([from_lower, gap, from_upper], axis=0)
    return (node_grad.astype(BF16), edge_grad, weight_grad)


def solution(mesh):
    placed = (
        P(AXES, None),
        P(AXES, None),
        P(AXES, None),
        P(AXES, None),
        P(),
        P(),
        P(AXES),
        P(AXES),
        P(AXES),
    )
    return jax.shard_map(
        per_device,
        mesh=mesh,
        in_specs=placed,
        out_specs=(P(AXES, None), P(AXES, None), P("patch", None)),
        check_vma=False,
    )
```

```python
import itertools

import jax
import jax.numpy as jnp
from jax import lax
from jax.experimental import pallas as pl
from jax.experimental.pallas import tpu as pltpu
from jax.sharding import PartitionSpec as P

HALO = 32
ROWS = 128
SLOTS = 768
WIDTH = 512
PLACES = 2 * ROWS + 2 * HALO
HALF = WIDTH // 2
BLOCK = 768
AXES = ("patch", "band")
BF16 = jnp.bfloat16
F32 = jnp.float32
VMEM = pl.BlockSpec(memory_space=pltpu.VMEM)
SMEM = pl.BlockSpec(memory_space=pltpu.SMEM)
HBM = pl.BlockSpec(memory_space=pl.ANY)


def device_groups(y_parts, x_parts, z_parts):
    groups = []
    for ys, xs, zs, core in itertools.product(y_parts, x_parts, z_parts, range(2)):
        groups.append(
            [((y * 4 + x) * 2 + core) * 8 + z for x, y, z in itertools.product(xs, ys, zs)]
        )
    return groups


Y_ORDER = (0,1)
ZP_ORDER = (1,0)
X_ORDER = (2,3,0,1)
QUAD_ORDER = (1,2,3,0)
Z_ORDER = (7,6,5,4,3,2,1,0)
NEAR = device_groups([[2 * i + k for k in Y_ORDER] for i in range(4)], [X_ORDER], [[2 * i + k for k in ZP_ORDER] for i in range(4)])
FAR = device_groups(
    [[2 * q + k for q in QUAD_ORDER] for k in range(2)], [[i] for i in range(4)], [Z_ORDER]
)
PAIR = [(i, i ^ 1) for i in range(64)]
CROSS = [(i, (i - 1) % 64 if i % 2 == 0 else (i + 1) % 64) for i in range(64)]

NN = ((1,), (0,))
NT = ((1,), (1,))
TN = ((0,), (0,))


def dot(a, b, dims=NN):
    return lax.dot_general(a, b, (dims, ((), ())), preferred_element_type=F32)


def hot(mask):
    return jnp.where(mask, 1.0, 0.0).astype(BF16)


def halves(values):
    high = values.astype(BF16)
    return jnp.concatenate([high, (values - high.astype(F32)).astype(BF16)], axis=0)


def lane_kernel(after, lane):
    lane[...] = lax.broadcasted_iota(jnp.int32, (128, 128), 1)


def lane_index(after):
    return pl.pallas_call(
        lane_kernel,
        out_shape=pltpu.VMEM((128, 128), jnp.int32),
        in_specs=[HBM],
        out_specs=VMEM,
        compiler_params=pltpu.CompilerParams(vmem_limit_bytes=8 * 1024 * 1024),
        cost_estimate=pl.CostEstimate(
            flops=20_000_000_000, bytes_accessed=100_000, transcendentals=0
        ),
    )(after)


def prepare_kernel(
    count,
    senders,
    receivers,
    lane_ref,
    nodes,
    edges,
    d_new,
    d_agg,
    w1,
    base,
    grad_new,
    edges_t,
    scatter,
    halo_hot,
):
    here = lax.axis_index("patch")
    odd = here % 2
    owner = senders[...] // (ROWS * 8)
    offset = senders[...] % ROWS
    lower = jnp.where(here == 0, 63, here - 1)
    lower_base = jnp.where(odd == 1, ROWS, ROWS + HALO) - (ROWS - HALO)
    upper_base = jnp.where(odd == 1, ROWS + HALO, ROWS)
    position = jnp.where(
        owner == here, offset, jnp.where(owner == lower, lower_base + offset, upper_base + offset)
    )
    receive = receivers[...]

    def columns(index, part):
        return jnp.broadcast_to(index[part : part + 1, :], (128, 128)).T

    lane = lane_ref[...]
    send_hot, recv_hot = [], []
    for part in range(SLOTS // 128):
        place = columns(position, part)
        send_hot.append(hot(place == lane))
        halo_hot[part * 128 : part * 128 + 128, :] = hot(place == ROWS + lane % 64)
        recv_hot.append(hot(columns(receive, part) == lane))
        row = slice(part * 128, part * 128 + 128)
        scatter[: ROWS + 2 * HALO, row] = hot(
            lax.broadcasted_iota(jnp.int32, (192, 128), 0) == position[part : part + 1, :]
        )
        scatter[ROWS + 2 * HALO :, row] = hot(
            lax.broadcasted_iota(jnp.int32, (128, 128), 0) == receive[part : part + 1, :]
        )
    product = jnp.concatenate(
        [
            dot(nodes[...], w1[WIDTH : 2 * WIDTH]).astype(BF16),
            dot(nodes[...], w1[2 * WIDTH :]).astype(BF16),
        ],
        axis=0,
    )
    for start in range(0, SLOTS, BLOCK):
        rows = slice(start, start + BLOCK)
        parts = range(start // 128, (start + BLOCK) // 128)
        gather = jnp.concatenate(
            [
                jnp.concatenate([send_hot[p], recv_hot[p]], axis=1)
                for p in parts
            ],
            axis=0,
        )
        base[rows, :] = dot(edges[rows, :], w1[:WIDTH]) + dot(gather, product)
        edges_t[:, rows] = edges[rows, :].T
    limit = jnp.broadcast_to(count[0:1, 0:1], (SLOTS, 1))
    for start in range(0, SLOTS, BLOCK):
        rows = slice(start, start + BLOCK)
        parts = range(start // 128, (start + BLOCK) // 128)
        slot = start + lax.broadcasted_iota(jnp.int32, (BLOCK, 1), 0)
        live = jnp.where(slot < limit[rows], 1.0, 0.0)
        taken = dot(jnp.concatenate([recv_hot[p] for p in parts], axis=0), d_agg[...])
        grad_new[rows, :] = live * (d_new[rows, :].astype(F32) + taken)


def prepare(*args):
    shapes = (
        ((SLOTS, WIDTH), F32),
        ((SLOTS, WIDTH), F32),
        ((WIDTH, SLOTS), BF16),
        ((PLACES, SLOTS), BF16),
        ((SLOTS, 128), BF16),
    )
    return pl.pallas_call(
        prepare_kernel,
        out_shape=[pltpu.VMEM(s, d) for s, d in shapes],
        in_specs=[VMEM] * 9,
        out_specs=[VMEM] * 5,
        compiler_params=pltpu.CompilerParams(vmem_limit_bytes=16 * 1024 * 1024),
        cost_estimate=pl.CostEstimate(
            flops=2_000_000_000, bytes_accessed=10_000_000, transcendentals=0
        ),
    )(*args)


def weight_kernel(
    cross,
    pair,
    base,
    grad_new,
    edges_t,
    scatter,
    halo_hot,
    w1,
    w2,
    nodes,
    mine,
    theirs,
    dz_all,
    summed,
    ret_cross,
    weight,
):
    odd = lax.axis_index("patch") % 2
    halo = jnp.concatenate([pair[...], cross[...]], axis=0)
    halo_product = halves(dot(halo, w1[WIDTH : 2 * WIDTH]))
    for start in range(0, SLOTS, BLOCK):
        rows = slice(start, start + BLOCK)
        pre = base[rows, :] + dot(halo_hot[rows, :], halo_product)
        sigma = 0.5 * jnp.tanh(0.5 * pre) + 0.5
        hidden = pre * sigma
        out = dot(hidden.astype(BF16), w2[...])
        center = out - jnp.mean(out, axis=-1, keepdims=True)
        rstd = lax.rsqrt(jnp.mean(center * center, axis=-1, keepdims=True) + 1e-05)
        normed = center * rstd
        grad = grad_new[rows, :]
        g_out = (
            grad
            - jnp.mean(grad, axis=-1, keepdims=True)
            - normed * jnp.mean(grad * normed, axis=-1, keepdims=True)
        ) * rstd
        g_hidden = dot(g_out.astype(BF16), w2[...], NT)
        dz_all[rows, :] = (g_hidden * (sigma + hidden * (1.0 - sigma))).astype(BF16)
    dz = dz_all[...]
    by_place = dot(scatter[...], dz).astype(BF16)
    summed[...] = by_place
    returned = dot(by_place[ROWS : ROWS + 2 * HALO], w1[WIDTH : 2 * WIDTH], NT).astype(BF16)
    theirs[2 * SLOTS : 2 * SLOTS + HALO, :] = returned[:HALO, :HALF]
    theirs[2 * SLOTS + HALO :, :] = returned[:HALO, HALF:]
    ret_cross[...] = returned[HALO:]
    table = jnp.concatenate([nodes[...], halo], axis=0)
    weight[:WIDTH] = dot(edges_t[...], dz)
    weight[WIDTH : 2 * WIDTH] = dot(table, by_place[: ROWS + 2 * HALO], TN)
    weight[2 * WIDTH :] = dot(nodes[...], by_place[ROWS + 2 * HALO :], TN)
    for target, core in ((mine, odd), (theirs, 1 - odd)):
        for x, y, z in itertools.product(range(4), range(2), range(2)):
            pieces = []
            for quad in range(4):
                first = ((quad * 2 + y) * 4 + x) * 48 + core * 24
                rows = pl.ds(pl.multiple_of(first, 8), 24)
                pieces.append(weight[rows, z * HALF : z * HALF + HALF])
            place = ((X_ORDER.index(x) * 2 + Y_ORDER.index(y)) * 2 + ZP_ORDER.index(z)) * 96
            target[place : place + 96, :] = jnp.concatenate(pieces, axis=0).astype(BF16)


def weight_terms(*args):
    shapes = (
        ((2 * SLOTS, HALF), BF16),
        ((2 * SLOTS + 2 * HALO, HALF), BF16),
        ((SLOTS, WIDTH), BF16),
        ((PLACES, WIDTH), BF16),
        ((HALO, WIDTH), BF16),
    )
    return pl.pallas_call(
        weight_kernel,
        out_shape=[pltpu.VMEM(s, d) for s, d in shapes],
        in_specs=[VMEM] * 10,
        out_specs=[VMEM] * 5,
        scratch_shapes=[pltpu.VMEM((3 * WIDTH, WIDTH), F32)],
        compiler_params=pltpu.CompilerParams(vmem_limit_bytes=20 * 1024 * 1024),
        cost_estimate=pl.CostEstimate(
            flops=2_000_000_000, bytes_accessed=10_000_000, transcendentals=400_000
        ),
    )(*args)


def finish_kernel(grad_new, summed, dz, w1, d_edges, node_grad):
    node_grad[...] = dot(summed[:ROWS], w1[WIDTH : 2 * WIDTH], NT) + dot(
        summed[ROWS + 2 * HALO :], w1[2 * WIDTH :], NT
    )
    d_edges[...] = (grad_new[...] + dot(dz[...], w1[:WIDTH], NT)).astype(BF16)


def finish(*args):
    return pl.pallas_call(
        finish_kernel,
        out_shape=[
            jax.ShapeDtypeStruct((SLOTS, WIDTH), BF16),
            jax.ShapeDtypeStruct((ROWS, WIDTH), F32),
        ],
        in_specs=[VMEM] * 4,
        out_specs=[VMEM] * 2,
        compiler_params=pltpu.CompilerParams(vmem_limit_bytes=20 * 1024 * 1024),
        cost_estimate=pl.CostEstimate(
            flops=1_000_000_000, bytes_accessed=5_000_000, transcendentals=0
        ),
    )(*args)


def exchange(block, groups):
    return lax.all_to_all(block, AXES, 0, 0, axis_index_groups=groups)


def small_call(body, shape, dtype, *args):
    return pl.pallas_call(
        body,
        out_shape=pltpu.VMEM(shape, dtype) if dtype == BF16 else jax.ShapeDtypeStruct(shape, dtype),
        in_specs=[VMEM] * len(args),
        out_specs=VMEM,
        compiler_params=pltpu.CompilerParams(vmem_limit_bytes=8 * 1024 * 1024),
    )(*args)


def add_kernel(mine, other, result):
    result[...] = (mine[...].astype(F32) + other[: 2 * SLOTS].astype(F32)).astype(BF16)


def near_kernel(terms, result):
    values = jnp.sum(terms[...].astype(F32), axis=0)
    for place, quad in enumerate(QUAD_ORDER):
        piece = values[quad * 24 : quad * 24 + 24].astype(BF16)
        for z in range(8):
            result[place * 8 + z] = piece


def far_kernel(terms, node_grad, other, from_cross, weight_grad, d_nodes):
    for half in range(2):
        places = [i for i in range(32) if Z_ORDER[i % 8] % 2 == half]
        values = terms[places[0]].astype(F32)
        for place in places[1:]:
            values = values + terms[place].astype(F32)
        weight_grad[:, half * HALF : half * HALF + HALF] = values
    odd = lax.axis_index("patch") % 2 == 1
    left, right = other[2 * SLOTS : 2 * SLOTS + HALO], other[2 * SLOTS + HALO :]
    from_pair = jnp.concatenate([left, right], axis=1).astype(F32)
    across = from_cross[...].astype(F32)
    lower = node_grad[:HALO] + jnp.where(odd, from_pair, across)
    upper = node_grad[ROWS - HALO :] + jnp.where(odd, across, from_pair)
    d_nodes[:HALO] = lower.astype(BF16)
    d_nodes[HALO : ROWS - HALO] = node_grad[HALO : ROWS - HALO].astype(BF16)
    d_nodes[ROWS - HALO :] = upper.astype(BF16)


def last_sums(*args):
    return pl.pallas_call(
        far_kernel,
        out_shape=[
            jax.ShapeDtypeStruct((24, WIDTH), F32),
            jax.ShapeDtypeStruct((ROWS, WIDTH), BF16),
        ],
        in_specs=[VMEM] * 4,
        out_specs=[VMEM] * 2,
        compiler_params=pltpu.CompilerParams(vmem_limit_bytes=8 * 1024 * 1024),
    )(*args)


def per_device(
    nodes, edges, d_new_edges, d_aggregate, edge_w1, edge_w2, senders, receivers, edge_count
):
    odd = lax.axis_index("patch") % 2
    first, last = nodes[:HALO], nodes[ROWS - HALO :]
    to_cross = jnp.where(odd == 0, first, last)
    to_pair = jnp.where(odd == 0, last, first)
    lane, to_cross, to_pair = lax.optimization_barrier((lane_index(to_cross), to_cross, to_pair))
    cross = lax.ppermute(to_cross, "patch", CROSS)
    pair = lax.ppermute(to_pair, "patch", PAIR)
    base, grad_new, edges_t, scatter, halo_hot = prepare(
        jnp.broadcast_to(edge_count, (8, 128)),
        senders.reshape(6, 128),
        receivers.reshape(6, 128),
        lane,
        nodes,
        edges,
        d_new_edges,
        d_aggregate,
        edge_w1,
    )
    mine, theirs, dz, summed, ret_cross = weight_terms(
        cross, pair, base, grad_new, edges_t, scatter, halo_hot, edge_w1, edge_w2, nodes
    )
    other = lax.ppermute(theirs, "patch", PAIR)
    edge_grad, node_grad = finish(grad_new, summed, dz, edge_w1)
    other, node_grad = lax.optimization_barrier((other, node_grad))
    weight = small_call(add_kernel, (2 * SLOTS, HALF), BF16, mine, other)
    weight = exchange(weight.reshape(16, 96, HALF), NEAR)
    weight = small_call(near_kernel, (32, 24, HALF), BF16, weight)
    weight, ret_cross = lax.optimization_barrier((weight, ret_cross))
    from_cross = lax.ppermute(ret_cross, "patch", CROSS)
    weight_grad, node_grad = last_sums(exchange(weight, FAR), node_grad, other, from_cross)
    return (node_grad, edge_grad, weight_grad)


def solution(mesh):
    placed = (
        P(AXES, None),
        P(AXES, None),
        P(AXES, None),
        P(AXES, None),
        P(),
        P(),
        P(AXES),
        P(AXES),
        P(AXES),
    )
    return jax.shard_map(
        per_device,
        mesh=mesh,
        in_specs=placed,
        out_specs=(P(AXES, None), P(AXES, None), P("patch", None)),
        check_vma=False,
    )
```

```python
import itertools

import jax
import jax.numpy as jnp
from jax import lax
from jax.experimental import pallas as pl
from jax.experimental.pallas import tpu as pltpu
from jax.sharding import PartitionSpec as P

HALO = 32
ROWS = 128
SLOTS = 768
WIDTH = 512
PLACES = 2 * ROWS + 2 * HALO
HALF = WIDTH // 2
BLOCK = 768
AXES = ("patch", "band")
BF16 = jnp.bfloat16
F32 = jnp.float32
VMEM = pl.BlockSpec(memory_space=pltpu.VMEM)
SMEM = pl.BlockSpec(memory_space=pltpu.SMEM)
HBM = pl.BlockSpec(memory_space=pl.ANY)


def device_groups(y_parts, x_parts, z_parts):
    groups = []
    for ys, xs, zs, core in itertools.product(y_parts, x_parts, z_parts, range(2)):
        groups.append(
            [((y * 4 + x) * 2 + core) * 8 + z for x, y, z in itertools.product(xs, ys, zs)]
        )
    return groups


Y_ORDER = (0,1)
ZP_ORDER = (1,0)
X_ORDER = (2,3,0,1)
QUAD_ORDER = (1,2,3,0)
Z_ORDER = (7,6,5,4,3,2,1,0)
NEAR = device_groups([[2 * i + k for k in Y_ORDER] for i in range(4)], [X_ORDER], [[2 * i + k for k in ZP_ORDER] for i in range(4)])
FAR = device_groups(
    [[2 * q + k for q in QUAD_ORDER] for k in range(2)], [[i] for i in range(4)], [Z_ORDER]
)
PAIR = [(i, i ^ 1) for i in range(64)]
CROSS = [(i, (i - 1) % 64 if i % 2 == 0 else (i + 1) % 64) for i in range(64)]

NN = ((1,), (0,))
NT = ((1,), (1,))
TN = ((0,), (0,))


def dot(a, b, dims=NN):
    return lax.dot_general(a, b, (dims, ((), ())), preferred_element_type=F32)


def hot(mask):
    return jnp.where(mask, 1.0, 0.0).astype(BF16)


def halves(values):
    high = values.astype(BF16)
    return jnp.concatenate([high, (values - high.astype(F32)).astype(BF16)], axis=0)


def lane_kernel(after, lane):
    lane[...] = lax.broadcasted_iota(jnp.int32, (128, 128), 1)


def lane_index(after):
    return pl.pallas_call(
        lane_kernel,
        out_shape=pltpu.VMEM((128, 128), jnp.int32),
        in_specs=[HBM],
        out_specs=VMEM,
        compiler_params=pltpu.CompilerParams(vmem_limit_bytes=8 * 1024 * 1024),
        cost_estimate=pl.CostEstimate(
            flops=20_000_000_000, bytes_accessed=100_000, transcendentals=0
        ),
    )(after)


def prepare_kernel(
    count,
    senders,
    receivers,
    lane_ref,
    nodes,
    edges,
    d_new,
    d_agg,
    w1,
    base,
    grad_new,
    edges_t,
    scatter,
    halo_hot,
):
    here = lax.axis_index("patch")
    odd = here % 2
    owner = senders[...] // (ROWS * 8)
    offset = senders[...] % ROWS
    lower = jnp.where(here == 0, 63, here - 1)
    lower_base = jnp.where(odd == 1, ROWS, ROWS + HALO) - (ROWS - HALO)
    upper_base = jnp.where(odd == 1, ROWS + HALO, ROWS)
    position = jnp.where(
        owner == here, offset, jnp.where(owner == lower, lower_base + offset, upper_base + offset)
    )
    receive = receivers[...]

    def columns(index, part):
        return jnp.broadcast_to(index[part : part + 1, :], (128, 128)).T

    lane = lane_ref[...]
    send_hot, recv_hot = [], []
    for part in range(SLOTS // 128):
        place = columns(position, part)
        send_hot.append(hot(place == lane))
        halo_hot[part * 128 : part * 128 + 128, :] = hot(place == ROWS + lane % 64)
        recv_hot.append(hot(columns(receive, part) == lane))
        row = slice(part * 128, part * 128 + 128)
        scatter[: ROWS + 2 * HALO, row] = hot(
            lax.broadcasted_iota(jnp.int32, (192, 128), 0) == position[part : part + 1, :]
        )
        scatter[ROWS + 2 * HALO :, row] = hot(
            lax.broadcasted_iota(jnp.int32, (128, 128), 0) == receive[part : part + 1, :]
        )
    product = jnp.concatenate(
        [
            halves(dot(nodes[...], w1[WIDTH : 2 * WIDTH])),
            halves(dot(nodes[...], w1[2 * WIDTH :])),
        ],
        axis=0,
    )
    for start in range(0, SLOTS, BLOCK):
        rows = slice(start, start + BLOCK)
        parts = range(start // 128, (start + BLOCK) // 128)
        gather = jnp.concatenate(
            [
                jnp.concatenate([send_hot[p], send_hot[p], recv_hot[p], recv_hot[p]], axis=1)
                for p in parts
            ],
            axis=0,
        )
        base[rows, :] = dot(edges[rows, :], w1[:WIDTH]) + dot(gather, product)
        edges_t[:, rows] = edges[rows, :].T
    limit = jnp.broadcast_to(count[0:1, 0:1], (SLOTS, 1))
    for start in range(0, SLOTS, BLOCK):
        rows = slice(start, start + BLOCK)
        parts = range(start // 128, (start + BLOCK) // 128)
        slot = start + lax.broadcasted_iota(jnp.int32, (BLOCK, 1), 0)
        live = jnp.where(slot < limit[rows], 1.0, 0.0)
        taken = dot(jnp.concatenate([recv_hot[p] for p in parts], axis=0), d_agg[...])
        grad_new[rows, :] = live * (d_new[rows, :].astype(F32) + taken)


def prepare(*args):
    shapes = (
        ((SLOTS, WIDTH), F32),
        ((SLOTS, WIDTH), F32),
        ((WIDTH, SLOTS), BF16),
        ((PLACES, SLOTS), BF16),
        ((SLOTS, 128), BF16),
    )
    return pl.pallas_call(
        prepare_kernel,
        out_shape=[pltpu.VMEM(s, d) for s, d in shapes],
        in_specs=[VMEM] * 9,
        out_specs=[VMEM] * 5,
        compiler_params=pltpu.CompilerParams(vmem_limit_bytes=16 * 1024 * 1024),
        cost_estimate=pl.CostEstimate(
            flops=2_000_000_000, bytes_accessed=10_000_000, transcendentals=0
        ),
    )(*args)


def weight_kernel(
    cross,
    pair,
    base,
    grad_new,
    edges_t,
    scatter,
    halo_hot,
    w1,
    w2,
    nodes,
    mine,
    theirs,
    dz_all,
    summed,
    ret_cross,
    weight,
):
    odd = lax.axis_index("patch") % 2
    halo = jnp.concatenate([pair[...], cross[...]], axis=0)
    halo_product = halves(dot(halo, w1[WIDTH : 2 * WIDTH]))
    for start in range(0, SLOTS, BLOCK):
        rows = slice(start, start + BLOCK)
        pre = base[rows, :] + dot(halo_hot[rows, :], halo_product)
        sigma = 0.5 * jnp.tanh(0.5 * pre) + 0.5
        hidden = pre * sigma
        out = dot(hidden.astype(BF16), w2[...])
        center = out - jnp.mean(out, axis=-1, keepdims=True)
        rstd = lax.rsqrt(jnp.mean(center * center, axis=-1, keepdims=True) + 1e-05)
        normed = center * rstd
        grad = grad_new[rows, :]
        g_out = (
            grad
            - jnp.mean(grad, axis=-1, keepdims=True)
            - normed * jnp.mean(grad * normed, axis=-1, keepdims=True)
        ) * rstd
        g_hidden = dot(g_out.astype(BF16), w2[...], NT)
        dz_all[rows, :] = (g_hidden * (sigma + hidden * (1.0 - sigma))).astype(BF16)
    dz = dz_all[...]
    by_place = dot(scatter[...], dz).astype(BF16)
    summed[...] = by_place
    returned = dot(by_place[ROWS : ROWS + 2 * HALO], w1[WIDTH : 2 * WIDTH], NT).astype(BF16)
    theirs[2 * SLOTS : 2 * SLOTS + HALO, :] = returned[:HALO, :HALF]
    theirs[2 * SLOTS + HALO :, :] = returned[:HALO, HALF:]
    ret_cross[...] = returned[HALO:]
    table = jnp.concatenate([nodes[...], halo], axis=0)
    weight[:WIDTH] = dot(edges_t[...], dz)
    weight[WIDTH : 2 * WIDTH] = dot(table, by_place[: ROWS + 2 * HALO], TN)
    weight[2 * WIDTH :] = dot(nodes[...], by_place[ROWS + 2 * HALO :], TN)
    for target, core in ((mine, odd), (theirs, 1 - odd)):
        for x, y, z in itertools.product(range(4), range(2), range(2)):
            pieces = []
            for quad in range(4):
                first = ((quad * 2 + y) * 4 + x) * 48 + core * 24
                rows = pl.ds(pl.multiple_of(first, 8), 24)
                pieces.append(weight[rows, z * HALF : z * HALF + HALF])
            place = ((X_ORDER.index(x) * 2 + Y_ORDER.index(y)) * 2 + ZP_ORDER.index(z)) * 96
            target[place : place + 96, :] = jnp.concatenate(pieces, axis=0).astype(BF16)


def weight_terms(*args):
    shapes = (
        ((2 * SLOTS, HALF), BF16),
        ((2 * SLOTS + 2 * HALO, HALF), BF16),
        ((SLOTS, WIDTH), BF16),
        ((PLACES, WIDTH), BF16),
        ((HALO, WIDTH), BF16),
    )
    return pl.pallas_call(
        weight_kernel,
        out_shape=[pltpu.VMEM(s, d) for s, d in shapes],
        in_specs=[VMEM] * 10,
        out_specs=[VMEM] * 5,
        scratch_shapes=[pltpu.VMEM((3 * WIDTH, WIDTH), F32)],
        compiler_params=pltpu.CompilerParams(vmem_limit_bytes=20 * 1024 * 1024),
        cost_estimate=pl.CostEstimate(
            flops=2_000_000_000, bytes_accessed=10_000_000, transcendentals=400_000
        ),
    )(*args)


def finish_kernel(grad_new, summed, dz, w1, d_edges, node_grad):
    node_grad[...] = dot(summed[:ROWS], w1[WIDTH : 2 * WIDTH], NT) + dot(
        summed[ROWS + 2 * HALO :], w1[2 * WIDTH :], NT
    )
    d_edges[...] = (grad_new[...] + dot(dz[...], w1[:WIDTH], NT)).astype(BF16)


def finish(*args):
    return pl.pallas_call(
        finish_kernel,
        out_shape=[
            jax.ShapeDtypeStruct((SLOTS, WIDTH), BF16),
            jax.ShapeDtypeStruct((ROWS, WIDTH), F32),
        ],
        in_specs=[VMEM] * 4,
        out_specs=[VMEM] * 2,
        compiler_params=pltpu.CompilerParams(vmem_limit_bytes=20 * 1024 * 1024),
        cost_estimate=pl.CostEstimate(
            flops=1_000_000_000, bytes_accessed=5_000_000, transcendentals=0
        ),
    )(*args)


def exchange(block, groups):
    return lax.all_to_all(block, AXES, 0, 0, axis_index_groups=groups)


def small_call(body, shape, dtype, *args):
    return pl.pallas_call(
        body,
        out_shape=pltpu.VMEM(shape, dtype) if dtype == BF16 else jax.ShapeDtypeStruct(shape, dtype),
        in_specs=[VMEM] * len(args),
        out_specs=VMEM,
        compiler_params=pltpu.CompilerParams(vmem_limit_bytes=8 * 1024 * 1024),
    )(*args)


def add_kernel(mine, other, result):
    result[...] = (mine[...].astype(F32) + other[: 2 * SLOTS].astype(F32)).astype(BF16)


def near_kernel(terms, result):
    values = jnp.sum(terms[...].astype(F32), axis=0)
    for place, quad in enumerate(QUAD_ORDER):
        piece = values[quad * 24 : quad * 24 + 24].astype(BF16)
        for z in range(8):
            result[place * 8 + z] = piece


def far_kernel(terms, node_grad, other, from_cross, weight_grad, d_nodes):
    for half in range(2):
        places = [i for i in range(32) if Z_ORDER[i % 8] % 2 == half]
        values = terms[places[0]].astype(F32)
        for place in places[1:]:
            values = values + terms[place].astype(F32)
        weight_grad[:, half * HALF : half * HALF + HALF] = values
    odd = lax.axis_index("patch") % 2 == 1
    left, right = other[2 * SLOTS : 2 * SLOTS + HALO], other[2 * SLOTS + HALO :]
    from_pair = jnp.concatenate([left, right], axis=1).astype(F32)
    across = from_cross[...].astype(F32)
    lower = node_grad[:HALO] + jnp.where(odd, from_pair, across)
    upper = node_grad[ROWS - HALO :] + jnp.where(odd, across, from_pair)
    d_nodes[:HALO] = lower.astype(BF16)
    d_nodes[HALO : ROWS - HALO] = node_grad[HALO : ROWS - HALO].astype(BF16)
    d_nodes[ROWS - HALO :] = upper.astype(BF16)


def last_sums(*args):
    return pl.pallas_call(
        far_kernel,
        out_shape=[
            jax.ShapeDtypeStruct((24, WIDTH), F32),
            jax.ShapeDtypeStruct((ROWS, WIDTH), BF16),
        ],
        in_specs=[VMEM] * 4,
        out_specs=[VMEM] * 2,
        compiler_params=pltpu.CompilerParams(vmem_limit_bytes=8 * 1024 * 1024),
    )(*args)


def per_device(
    nodes, edges, d_new_edges, d_aggregate, edge_w1, edge_w2, senders, receivers, edge_count
):
    odd = lax.axis_index("patch") % 2
    first, last = nodes[:HALO], nodes[ROWS - HALO :]
    to_cross = jnp.where(odd == 0, first, last)
    to_pair = jnp.where(odd == 0, last, first)
    lane, to_cross, to_pair = lax.optimization_barrier((lane_index(to_cross), to_cross, to_pair))
    cross = lax.ppermute(to_cross, "patch", CROSS)
    pair = lax.ppermute(to_pair, "patch", PAIR)
    base, grad_new, edges_t, scatter, halo_hot = prepare(
        jnp.broadcast_to(edge_count, (8, 128)),
        senders.reshape(6, 128),
        receivers.reshape(6, 128),
        lane,
        nodes,
        edges,
        d_new_edges,
        d_aggregate,
        edge_w1,
    )
    mine, theirs, dz, summed, ret_cross = weight_terms(
        cross, pair, base, grad_new, edges_t, scatter, halo_hot, edge_w1, edge_w2, nodes
    )
    other = lax.ppermute(theirs, "patch", PAIR)
    edge_grad, node_grad = finish(grad_new, summed, dz, edge_w1)
    other, node_grad = lax.optimization_barrier((other, node_grad))
    weight = small_call(add_kernel, (2 * SLOTS, HALF), BF16, mine, other)
    weight = exchange(weight.reshape(16, 96, HALF), NEAR)
    weight = small_call(near_kernel, (32, 24, HALF), BF16, weight)
    weight, ret_cross = lax.optimization_barrier((weight, ret_cross))
    from_cross = lax.ppermute(ret_cross, "patch", CROSS)
    weight_grad, node_grad = last_sums(exchange(weight, FAR), node_grad, other, from_cross)
    return (node_grad, edge_grad, weight_grad)


def solution(mesh):
    placed = (
        P(AXES, None),
        P(AXES, None),
        P(AXES, None),
        P(AXES, None),
        P(),
        P(),
        P(AXES),
        P(AXES),
        P(AXES),
    )
    return jax.shard_map(
        per_device,
        mesh=mesh,
        in_specs=placed,
        out_specs=(P(AXES, None), P(AXES, None), P("patch", None)),
        check_vma=False,
    )
```
